256 devices in a mesh: layer: 2 (over core), row: 32 (over x, z), col: 4 (over y).
Axes of the slice: x: 4, y: 4, z: 8, core: 2. Of those that a mesh axis runs over, the one named last changes fastest.
Arguments:
- tile_values: bfloat16 [2, 32, 4, 256, 128, 128], P('layer', 'row', 'col'), may hold values from -0.5 to 0.5
- tile_rows: int32 [2, 32, 4, 256], P('layer', 'row', 'col'), may hold values from 0 to 31
- tile_cols: int32 [2, 32, 4, 256], P('layer', 'row', 'col'), may hold values from 0 to 63
- tile_count: int32 [2, 32, 4], P('layer', 'row', 'col'), may hold values from 64 to 256, as said below
- start_panel: bfloat16 [32768, 128], P('col'), may hold values from -6 to 6
Outputs:
- caller_panel: bfloat16 [32, 4096, 128], P('row', ('layer', 'col'))
- dest_panel: bfloat16 [4, 8192, 128], P('col', ('layer', 'row'))
The draws below stay inside these ranges and needn't reach their ends.
Inputs may be any that keep to these rules, and one draw needn't show every extreme that they name: tile_count reaches 256 on some device.
All inputs are finite; a program needn't handle non-finite values.
Results may differ from the reference program's by a relative error of at most 0.0049.
Values may be sent and summed in bfloat16 or wider, within the bound.
No kernel may reach another device: no remote copies, remote signals or barrier semaphores. Data moves between devices by JAX's collectives and lax.ppermute only.
A program may use at most 128 MiB of HBM per device.

```python
import math
import jax
import jax.numpy as jnp
import numpy as np
from jax import lax

TILE = 128
RANK = 128
CTILES = 32
DTILES = 64
NT_DEV = 256
NDST = 32768
N_LAYER = 2
N_ROW = 32
N_COL = 4


def draw_tile_count(key, part):
    first_key, second_key = jax.random.split(jax.random.fold_in(key, 7))
    total = N_LAYER * N_ROW * N_COL
    counts = jax.random.randint(first_key, (total,), NT_DEV // 4, NT_DEV + 1)
    target = jax.random.randint(second_key, (), 0, total)
    counts = counts.at[target].set(NT_DEV)
    return counts.reshape(N_LAYER, N_ROW, N_COL).astype(jnp.int32)


def with_ends(entries, key, low, largest):
    spot = [jax.random.randint(jax.random.fold_in(key, axis), (), 0, length) for axis, length in enumerate(entries.shape)]
    main_axis = entries.shape.index(max(entries.shape))
    next_to = spot[:main_axis] + [(spot[main_axis] + 1) % entries.shape[main_axis]] + spot[main_axis + 1:]
    return entries.at[tuple(spot)].set(low).at[tuple(next_to)].set(largest)


def shard_levels(own_key, shape, cuts, least, high):
    def one(position, shards_of):
        heights = jax.random.uniform(jax.random.fold_in(jax.random.fold_in(own_key, 6), position), (shards_of,), jnp.float32, least / len(cuts), high / len(cuts))
        return jnp.repeat(jnp.exp(heights), shape[position] // shards_of).reshape((-1,) + (1,) * (len(shape) - position - 1))

    gain = one(*cuts[0])
    for cut in cuts[1:]:
        gain = gain * one(*cut)
    return gain


def cumulative_ranks(count, lean):
    portions = [(1 << 20) // math.isqrt(rank ** lean) + 1 for rank in range(1, count + 1)]
    scale = 1 + sum(portions) // (1 << 30)
    return np.cumsum(np.array([max(1, weight // scale) for weight in portions]))


def ranked_ids(own_key, extent, count, lean):
    listing = cumulative_ranks(count, lean)
    pick = jax.random.randint(jax.random.fold_in(own_key, 1), extent, 0, int(listing[count - 1]))
    standing = jnp.searchsorted(jnp.asarray(listing, jnp.int32), pick, side="right")
    return jax.random.permutation(jax.random.fold_in(own_key, 2), count)[standing].astype(jnp.int32)


def bell_draw(stream_key, dims, scale, limit, pieces=(), dtype=jnp.bfloat16):
    drawn = jax.random.normal(stream_key, dims, jnp.float32) * scale
    if len(pieces) > 0:
        drawn = shard_levels(stream_key, dims, pieces, -0.22, 0.18) * drawn
    return jnp.clip(drawn, min=-limit, max=limit).astype(dtype)


def setup_inputs(seed: int = 0) -> dict:
    key_list = jax.random.split(jax.random.key(seed), 6)
    return {
        "tile_values": bell_draw(key_list[0], (N_LAYER, N_ROW, N_COL, NT_DEV, TILE, TILE), TILE ** -0.5, 0.5, ((0, 2), (1, 32), (2, 4))),
        "tile_rows": with_ends(ranked_ids(key_list[1], (N_LAYER, N_ROW, N_COL, NT_DEV), CTILES, 2), jax.random.fold_in(key_list[1], 3), 0, CTILES - 1).astype(jnp.int32),
        "tile_cols": with_ends(jax.random.randint(key_list[2], (N_LAYER, N_ROW, N_COL, NT_DEV), 0, DTILES), jax.random.fold_in(key_list[2], 1), 0, DTILES - 1).astype(jnp.int32),
        "tile_count": draw_tile_count(jax.random.fold_in(key_list[5], 71), 0),
        "start_panel": bell_draw(key_list[4], (NDST, RANK), 1.0, 6.0, ((0, 4),)),
    }


EPS = 1e-06

def forward_block(tiles, rows, cols, count, panel):
    live = jnp.arange(tiles.shape[0]) < count
    dense = jnp.where(live[:, None, None], tiles.astype(jnp.float32), 0.0)
    picked = panel.astype(jnp.float32).reshape(DTILES, TILE, RANK)[cols]
    prods = jnp.einsum('tij,tjr->tir', dense, picked, precision=lax.Precision.HIGHEST)
    sums = jax.ops.segment_sum(prods, rows, num_segments=CTILES)
    return sums.reshape(CTILES * TILE, RANK)

def backward_block(tiles, rows, cols, count, panel):
    live = jnp.arange(tiles.shape[0]) < count
    dense = jnp.where(live[:, None, None], tiles.astype(jnp.float32), 0.0)
    picked = panel.astype(jnp.float32).reshape(CTILES, TILE, RANK)[rows]
    prods = jnp.einsum('tij,tir->tjr', dense, picked, precision=lax.Precision.HIGHEST)
    sums = jax.ops.segment_sum(prods, cols, num_segments=DTILES)
    return sums.reshape(DTILES * TILE, RANK)

def caller_pass(tile_values, tile_rows, tile_cols, tile_count, dest_blocks):
    total = jnp.zeros((N_ROW, CTILES * TILE, RANK), jnp.float32)
    for layer_idx in range(N_LAYER):
        for col_idx in range(N_COL):
            panel = dest_blocks[col_idx]
            total = total + lax.map(lambda xs: forward_block(xs[0], xs[1], xs[2], xs[3], panel), (tile_values[layer_idx, :, col_idx], tile_rows[layer_idx, :, col_idx], tile_cols[layer_idx, :, col_idx], tile_count[layer_idx, :, col_idx]))
    return total

def normalize(values):
    scale = lax.rsqrt(lax.optimization_barrier(jnp.mean(values * values, axis=(0, 1))) + EPS)
    return (values * scale).astype(jnp.bfloat16)

def reference(tile_values, tile_rows, tile_cols, tile_count, start_panel):
    start_blocks = start_panel.reshape(N_COL, DTILES * TILE, RANK)
    first = caller_pass(tile_values, tile_rows, tile_cols, tile_count, start_blocks)
    first_rounded = first.astype(jnp.bfloat16)
    backs = []
    for col_idx in range(N_COL):
        acc = jnp.zeros((DTILES * TILE, RANK), jnp.float32)
        for layer_idx in range(N_LAYER):
            parts = lax.map(lambda xs: backward_block(xs[0], xs[1], xs[2], xs[3], xs[4]), (tile_values[layer_idx, :, col_idx], tile_rows[layer_idx, :, col_idx], tile_cols[layer_idx, :, col_idx], tile_count[layer_idx, :, col_idx], first_rounded))
            acc = acc + lax.optimization_barrier(jnp.sum(parts, axis=0))
        backs.append(acc)
    dest_panel = normalize(jnp.stack(backs))
    last = caller_pass(tile_values, tile_rows, tile_cols, tile_count, dest_panel)
    return (last.astype(jnp.bfloat16), dest_panel)
```

```python
import functools

import jax
import jax.numpy as jnp
from jax import lax
from jax.experimental import pallas as pl
from jax.experimental.pallas import tpu as pltpu
from jax.sharding import Mesh
from jax.sharding import PartitionSpec as P

TILE = 128
RANK = 128
CTILES = 32
DTILES = 64
NX = 4
NZ = 8
NCOL = 4
NDST = 32768
BLOCK = 64
UNROLL = 16
EPS = 1e-06

F32 = jnp.float32
BF16 = jnp.bfloat16
CORE, XPOS, ZPOS, COL = 0, 1, 2, 3

SMEM = pl.BlockSpec(memory_space=pltpu.SMEM)
VMEM = pl.BlockSpec(memory_space=pltpu.VMEM)
PARAMS = pltpu.CompilerParams(vmem_limit_bytes=40 * 2**20)


def tiles_of(n, dtype):
    return jax.ShapeDtypeStruct((n, TILE, RANK), dtype)


def each(n, body):
    def step(i, carry):
        body(i)
        return carry

    lax.fori_loop(0, n, step, 0)


def accumulate(step, dst, src, count, tiles_ref, panel, acc, dump, tile_left):
    live = count[0]
    left = jnp.minimum(live - step * BLOCK, BLOCK)

    def group(g, carry):
        for j in range(UNROLL):
            k = g * UNROLL + j
            t = step * BLOCK + k
            d = jnp.where(t < live, dst[t], dump)
            tile, block = tiles_ref[k], panel[src[t]]
            a, b = (tile, block) if tile_left else (block, tile)
            acc[d] += jnp.dot(a, b, preferred_element_type=F32)
        return carry

    lax.fori_loop(0, (left + UNROLL - 1) // UNROLL, group, 0)


def split(ids, acc, keep, send, half):
    core = ids[CORE]

    def one(i):
        keep[i] = acc[core * half + i]
        send[i] = acc[(1 - core) * half + i].astype(BF16)

    each(half, one)


def place(ids, parts, panel, axis, n, per, half):
    core, me = ids[CORE], ids[axis]
    for side in range(2):
        base = jnp.where(side == 0, core, 1 - core) * half
        for k in range(n):
            at = base + lax.rem(me + n - k, n) * per
            part = parts[side * n + k]

            def one(i):
                panel[at + i] = part[i]

            each(per, one)


def zero(acc):
    def one(i):
        acc[i] = jnp.zeros((TILE, RANK), F32)

    each(acc.shape[0], one)


def first_kernel(dst, src, count, ids, tiles_ref, panel, keep, send, acc):
    step = pl.program_id(0)

    @pl.when(step == 0)
    def _():
        zero(acc)

    accumulate(step, dst, src, count, tiles_ref, panel, acc, CTILES, True)

    @pl.when(step == pl.num_programs(0) - 1)
    def _():
        split(ids, acc, keep, send, CTILES // 2)


def back_kernel(dst, src, count, ids, tiles_ref, *refs):
    parts, (keep, send, panel, acc) = refs[: 2 * NCOL], refs[2 * NCOL :]
    step = pl.program_id(0)

    @pl.when(step == 0)
    def _():
        zero(acc)
        place(ids, parts, panel, COL, NCOL, CTILES // 2 // NCOL, CTILES // 2)

    accumulate(step, dst, src, count, tiles_ref, panel, acc, DTILES, False)

    @pl.when(step == pl.num_programs(0) - 1)
    def _():
        split(ids, acc, keep, send, DTILES // 2)


def last_kernel(dst, src, count, ids, tiles_ref, *refs):
    parts, (keep, send, squares, panel, acc) = refs[: 2 * NX], refs[2 * NX :]
    step = pl.program_id(0)

    @pl.when(step == 0)
    def _():
        zero(acc)
        place(ids, parts, panel, XPOS, NX, NZ, DTILES // 2)

    accumulate(step, dst, src, count, tiles_ref, panel, acc, CTILES, True)

    @pl.when(step == pl.num_programs(0) - 1)
    def _():
        split(ids, acc, keep, send, CTILES // 2)

        def one(i, total):
            block = panel[i].astype(F32)
            return total + jnp.sum((block * block).reshape(TILE // 8, 8, RANK), axis=0)

        squares[...] = lax.fori_loop(0, DTILES, one, jnp.zeros((8, RANK), F32))


def tile_pass(kernel, dst, src, count, ids, tiles, parts, n_acc, panel_tiles, extra, name):
    whole = lambda n: pl.BlockSpec((n, TILE, RANK), lambda i, *_: (0, 0, 0))
    half = n_acc // 2
    scratch = [pltpu.VMEM((n_acc + 1, TILE, RANK), F32)]
    if panel_tiles:
        scratch.insert(0, pltpu.VMEM((panel_tiles, TILE, RANK), BF16))
    return pl.pallas_call(
        kernel,
        grid_spec=pltpu.PrefetchScalarGridSpec(
            num_scalar_prefetch=4,
            grid=(tiles.shape[0] // BLOCK,),
            in_specs=[
                pl.BlockSpec(
                    (BLOCK, TILE, TILE),
                    lambda i, dst, src, count, ids: (jnp.minimum(i, (count[0] - 1) // BLOCK), 0, 0),
                )
            ]
            + [whole(p.shape[0]) for p in parts],
            out_specs=[whole(half), whole(half)]
            + [pl.BlockSpec(e.shape, lambda i, *_: (0, 0)) for e in extra],
            scratch_shapes=scratch,
        ),
        out_shape=[tiles_of(half, F32), tiles_of(half, BF16)] + extra,
        compiler_params=PARAMS,
        name=name,
    )(dst, src, count, ids, tiles, *parts)


def pair_kernel(ids, keep, got, own, *sends, axis, n, per):
    me = ids[axis]
    for k in range(n):
        base = lax.rem(me + k, n) * per

        def one(i):
            total = keep[base + i] + got[base + i].astype(F32)
            if k == 0:
                own[i] = total
            else:
                sends[k - 1][i] = total.astype(BF16)

        each(per, one)


def pair_sum(ids, keep, got, axis, n, per, name):
    return pl.pallas_call(
        functools.partial(pair_kernel, axis=axis, n=n, per=per),
        in_specs=[SMEM, VMEM, VMEM],
        out_specs=[VMEM] * n,
        out_shape=[tiles_of(per, F32)] + [tiles_of(per, BF16)] * (n - 1),
        compiler_params=PARAMS,
        name=name,
    )(ids, keep, got)


def caller_kernel(own, a, b, c, out):
    def one(i):
        total = own[i] + a[i].astype(F32) + b[i].astype(F32) + c[i].astype(F32)
        out[i] = total.astype(BF16).astype(F32).T.astype(BF16)

    each(own.shape[0], one)


def row_kernel(own, a, b, c, out):
    def one(i):
        total = own[i] + a[i].astype(F32) + b[i].astype(F32) + c[i].astype(F32)
        out[i] = total.astype(BF16)

    each(own.shape[0], one)


def four_sum(kernel, own, got, name):
    return pl.pallas_call(
        kernel,
        in_specs=[VMEM] * 4,
        out_specs=VMEM,
        out_shape=tiles_of(own.shape[0], BF16),
        compiler_params=PARAMS,
        name=name,
    )(own, *got)


def share_kernel(got, share, copies):
    total = got[0].astype(F32)
    for k in range(1, NZ):
        total += got[k].astype(F32)
    total = total.T
    share[...] = total
    for k in range(NZ):
        copies[k] = total.astype(BF16)


def last_pair_kernel(ids, keep, got, squares, own, *sends):
    me = ids[COL]
    per = CTILES // 2 // NCOL
    total = jnp.sum(squares[...], axis=0, keepdims=True)
    high = total.astype(BF16).astype(F32)
    middle = (total - high).astype(BF16).astype(F32)
    low = total - high - middle
    row = lax.broadcasted_iota(jnp.int32, (16, RANK), 0)
    coded = jnp.where(row == 0, high, jnp.where(row == 1, middle, jnp.where(row == 2, low, 0.0)))
    for k in range(NCOL):
        base = lax.rem(me + k, NCOL) * per
        if k:
            sends[k - 1][pl.ds(per * TILE, 16), :] = coded.astype(BF16)
        for i in range(per):
            part = keep[base + i] + got[base + i].astype(F32)
            if k == 0:
                own[i] = part
            else:
                sends[k - 1][pl.ds(i * TILE, TILE), :] = part.astype(BF16)


def final_kernel(own, squares, share, a, b, c, caller, dest):
    per = CTILES // 2 // NCOL
    total = jnp.sum(squares[...], axis=0, keepdims=True)
    for got in (a, b, c):
        total += jnp.sum(got[pl.ds(per * TILE, 16), :].astype(F32), axis=0, keepdims=True)
    scale = lax.rsqrt(total / NDST + EPS)
    dest[...] = (share[...] * scale).astype(BF16)
    for i in range(per):
        at = pl.ds(i * TILE, TILE)
        part = own[i] + a[at, :].astype(F32) + b[at, :].astype(F32) + c[at, :].astype(F32)
        caller[at, :] = (part * scale).astype(BF16)


def shifted(value, axis, k, n):
    return lax.ppermute(value, axis, [(i, (i + k) % n) for i in range(n)])


def swap(value):
    return lax.ppermute(value, "layer", [(0, 1), (1, 0)])


def exchange(values, axis, n):
    return [shifted(v, axis, k + 1, n) for k, v in enumerate(values)]


def gather(value, axis, n):
    mine = [value] + [shifted(value, axis, k, n) for k in range(1, n)]
    return mine + [swap(v) for v in mine]


def on_device(tile_values, tile_rows, tile_cols, tile_count, start_panel):
    tiles = tile_values[0, 0, 0]
    rows = tile_rows[0, 0, 0]
    cols = tile_cols[0, 0, 0]
    count = tile_count[0, 0]
    ids = jnp.stack([lax.axis_index(a) for a in ("layer", "x", "z", "col")]).astype(jnp.int32)
    start = start_panel.reshape(DTILES, TILE, RANK)
    quarter = CTILES // 2 // NCOL

    keep, send = tile_pass(first_kernel, rows, cols, count, ids, tiles, [start], CTILES, 0, [], "first_pass")
    own, *sends = pair_sum(ids, keep, swap(send), COL, NCOL, quarter, "first_pair")
    part = four_sum(caller_kernel, own, exchange(sends, "col", NCOL), "first_sum")
    parts = gather(part, "col", NCOL)

    keep, send = tile_pass(back_kernel, cols, rows, count, ids, tiles, parts, DTILES, CTILES, [], "back_pass")
    own, *sends = pair_sum(ids, keep, swap(send), XPOS, NX, NZ, "back_pair")
    part = four_sum(row_kernel, own, exchange(sends, "x", NX), "back_sum")
    got = lax.all_to_all(part, "z", split_axis=0, concat_axis=0, tiled=True)
    share, copies = pl.pallas_call(
        share_kernel,
        in_specs=[VMEM],
        out_specs=[VMEM, VMEM],
        out_shape=[jax.ShapeDtypeStruct((TILE, RANK), F32), tiles_of(NZ, BF16)],
        compiler_params=PARAMS,
        name="share_sum",
    )(got)
    part = lax.all_to_all(copies, "z", split_axis=0, concat_axis=0, tiled=True)
    parts = gather(part, "x", NX)

    keep, send, squares = tile_pass(
        last_kernel, rows, cols, count, ids, tiles, parts, CTILES, DTILES,
        [jax.ShapeDtypeStruct((8, RANK), F32)], "last_pass",
    )
    chunk = jax.ShapeDtypeStruct((quarter * TILE + 16, RANK), BF16)
    own, *sends = pl.pallas_call(
        last_pair_kernel,
        in_specs=[SMEM, VMEM, VMEM, VMEM],
        out_specs=[VMEM] * NCOL,
        out_shape=[tiles_of(quarter, F32)] + [chunk] * (NCOL - 1),
        compiler_params=PARAMS,
        name="last_pair",
    )(ids, keep, swap(send), squares)
    got = exchange(sends, "col", NCOL)
    caller, dest = pl.pallas_call(
        final_kernel,
        in_specs=[VMEM] * 6,
        out_specs=[VMEM, VMEM],
        out_shape=[
            jax.ShapeDtypeStruct((quarter * TILE, RANK), BF16),
            jax.ShapeDtypeStruct((TILE, RANK), BF16),
        ],
        compiler_params=PARAMS,
        name="final",
    )(own, squares, share, *got)
    return caller[None], dest[None]


def solution(mesh):
    fine = Mesh(mesh.devices.reshape(2, NX, NZ, NCOL), ("layer", "x", "z", "col"))
    row = ("x", "z")
    placed = (
        P("layer", row, "col", None, None, None),
        P("layer", row, "col", None),
        P("layer", row, "col", None),
        P("layer", row, "col"),
        P("col", None),
    )
    return jax.shard_map(
        on_device,
        mesh=fine,
        in_specs=placed,
        out_specs=(P(row, ("layer", "col"), None), P("col", ("layer", "x", "z"), None)),
        check_vma=False,
    )
```

```python
import jax
import jax.numpy as jnp
from jax import lax
from jax.experimental import pallas as pl
from jax.experimental.pallas import tpu as pltpu
from jax.sharding import Mesh
from jax.sharding import PartitionSpec as P

TILE = 128
RANK = 128
CTILES = 32
DTILES = 64
NX = 4
NZ = 8
NCOL = 4
NDST = 32768
BLOCK = 64
UNROLL = 32
EPS = 1e-06

F32 = jnp.float32
BF16 = jnp.bfloat16
CORE, XPOS, COL = 0, 1, 2

SMEM = pl.BlockSpec(memory_space=pltpu.SMEM)
VMEM = pl.BlockSpec(memory_space=pltpu.VMEM)
HBM = pl.BlockSpec(memory_space=pltpu.HBM)
PARAMS = pltpu.CompilerParams(vmem_limit_bytes=40 * 2**20)


def tiles_of(n, dtype):
    return jax.ShapeDtypeStruct((n, TILE, RANK), dtype)


def each(n, body):
    def step(i, carry):
        body(i)
        return carry

    lax.fori_loop(0, n, step, 0)


def accumulate(first, size, dst, src, count, tiles, panel, acc, dump, tile_left):
    live = count[0]
    left = jnp.clip(live - first, 0, size)

    def group(g, carry):
        for j in range(UNROLL):
            t = first + g * UNROLL + j
            d = jnp.where(t < live, dst[t], dump)
            tile, block = tiles[t], panel[src[t]]
            a, b = (tile, block) if tile_left else (block, tile)
            acc[d] += jnp.dot(a, b, preferred_element_type=F32)
        return carry

    lax.fori_loop(0, (left + UNROLL - 1) // UNROLL, group, 0)


def split(ids, acc, keep, send, half):
    core = ids[CORE]

    def one(i):
        keep[i] = acc[core * half + i]
        send[i] = acc[(1 - core) * half + i].astype(BF16)

    each(half, one)


def zero(acc):
    def one(i):
        acc[i] = jnp.zeros((TILE, RANK), F32)

    each(acc.shape[0], one)


def place(ids, parts, panel, axis, n, per):
    core, me = ids[CORE], ids[axis]
    for side in range(2):
        base = jnp.where(side == 0, core, 1 - core) * (n * per)
        for k in range(n):
            at = base + lax.rem(me + n - k, n) * per
            part = parts[side * n + k]

            def one(i):
                panel[at + i] = part[i]

            each(per, one)


def first_kernel(dst_hbm, src_hbm, count, ids, tiles_hbm, panel_hbm, keep, send, tiles, dst, src, panel, acc, sems):
    n_blocks = tiles.shape[0] // BLOCK
    lists = [
        pltpu.make_async_copy(dst_hbm, dst, sems.at[0]),
        pltpu.make_async_copy(src_hbm, src, sems.at[1]),
        pltpu.make_async_copy(panel_hbm, panel, sems.at[2]),
    ]
    blocks = [
        pltpu.make_async_copy(
            tiles_hbm.at[pl.ds(i * BLOCK, BLOCK)], tiles.at[pl.ds(i * BLOCK, BLOCK)], sems.at[3 + i]
        )
        for i in range(n_blocks)
    ]
    for copy in lists + blocks:
        copy.start()
    zero(acc)
    for copy in lists:
        copy.wait()
    for i in range(n_blocks):
        blocks[i].wait()
        accumulate(i * BLOCK, BLOCK, dst, src, count, tiles, panel, acc, CTILES, True)
    split(ids, acc, keep, send, CTILES // 2)


def in_hbm(value):
    return pltpu.with_memory_space_constraint(value, pltpu.HBM)


def first_pass(rows, cols, count, ids, tiles, start):
    return pl.pallas_call(
        first_kernel,
        in_specs=[HBM, HBM, SMEM, SMEM, HBM, HBM],
        out_specs=[VMEM] * 3,
        out_shape=[tiles_of(CTILES // 2, F32), tiles_of(CTILES // 2, BF16), tiles_of(tiles.shape[0], BF16)],
        scratch_shapes=[
            pltpu.SMEM(rows.shape, jnp.int32),
            pltpu.SMEM(cols.shape, jnp.int32),
            pltpu.VMEM(start.shape, BF16),
            pltpu.VMEM((CTILES + 1, TILE, RANK), F32),
            pltpu.SemaphoreType.DMA((3 + tiles.shape[0] // BLOCK,)),
        ],
        compiler_params=pltpu.CompilerParams(vmem_limit_bytes=40 * 2**20),
        name="first_pass",
    )(*(in_hbm(v) for v in (rows, cols)), count, ids, *(in_hbm(v) for v in (tiles, start)))


def back_kernel(dst, src, count, ids, tiles, *refs):
    parts, (keep, send, panel, acc) = refs[: 2 * NCOL], refs[2 * NCOL :]
    zero(acc)
    place(ids, parts, panel, COL, NCOL, CTILES // 2 // NCOL)
    accumulate(0, tiles.shape[0], dst, src, count, tiles, panel, acc, DTILES, False)
    split(ids, acc, keep, send, DTILES // 2)


def last_kernel(dst, src, count, ids, tiles, *refs):
    parts, (keep, send, squares, panel, acc) = refs[: 2 * NX], refs[2 * NX :]
    zero(acc)
    place(ids, parts, panel, XPOS, NX, NZ)
    accumulate(0, tiles.shape[0], dst, src, count, tiles, panel, acc, CTILES, True)
    split(ids, acc, keep, send, CTILES // 2)

    def one(i, total):
        block = panel[i].astype(F32)
        return total + jnp.sum((block * block).reshape(TILE // 8, 8, RANK), axis=0)

    squares[...] = lax.fori_loop(0, DTILES, one, jnp.zeros((8, RANK), F32))


def tile_pass(kernel, dst, src, count, ids, tiles, parts, n_acc, panel_tiles, extra, name):
    half = n_acc // 2
    return pl.pallas_call(
        kernel,
        in_specs=[SMEM] * 4 + [VMEM] * (1 + len(parts)),
        out_specs=[VMEM] * (2 + len(extra)),
        out_shape=[tiles_of(half, F32), tiles_of(half, BF16)] + extra,
        scratch_shapes=[
            pltpu.VMEM((panel_tiles, TILE, RANK), BF16),
            pltpu.VMEM((n_acc + 1, TILE, RANK), F32),
        ],
        compiler_params=PARAMS,
        name=name,
    )(dst, src, count, ids, tiles, *parts)


def first_pair_kernel(ids, keep, got, own, *sends):
    me = ids[COL]
    per = own.shape[0]
    for k in range(NCOL):
        base = lax.rem(me + k, NCOL) * per

        def one(i):
            total = keep[base + i] + got[base + i].astype(F32)
            if k == 0:
                own[i] = total
            else:
                sends[k - 1][i] = total.astype(BF16)

        each(per, one)


def back_pair_kernel(keep, got, out):
    def one(i):
        out[i] = (keep[i] + got[i].astype(F32)).astype(BF16)

    each(out.shape[0], one)


def caller_kernel(own, a, b, c, out):
    def one(i):
        total = own[i] + a[i].astype(F32) + b[i].astype(F32) + c[i].astype(F32)
        out[i] = total.astype(BF16).astype(F32).T.astype(BF16)

    each(own.shape[0], one)


def share_kernel(got, share, copies):
    total = got[0].astype(F32)
    for k in range(1, NX * NZ):
        total += got[k].astype(F32)
    total = total.T
    share[...] = total
    for k in range(NZ):
        copies[k] = total.astype(BF16)


def last_pair_kernel(ids, keep, got, squares, own, *sends):
    me = ids[COL]
    per = CTILES // 2 // NCOL
    total = jnp.sum(squares[...], axis=0, keepdims=True)
    high = total.astype(BF16).astype(F32)
    middle = (total - high).astype(BF16).astype(F32)
    low = total - high - middle
    row = lax.broadcasted_iota(jnp.int32, (16, RANK), 0)
    coded = jnp.where(row == 0, high, jnp.where(row == 1, middle, jnp.where(row == 2, low, 0.0)))
    for k in range(NCOL):
        base = lax.rem(me + k, NCOL) * per
        if k:
            sends[k - 1][pl.ds(per * TILE, 16), :] = coded.astype(BF16)
        for i in range(per):
            part = keep[base + i] + got[base + i].astype(F32)
            if k == 0:
                own[i] = part
            else:
                sends[k - 1][pl.ds(i * TILE, TILE), :] = part.astype(BF16)


def final_kernel(own, squares, share, a, b, c, caller, dest):
    per = CTILES // 2 // NCOL
    total = jnp.sum(squares[...], axis=0, keepdims=True)
    for got in (a, b, c):
        total += jnp.sum(got[pl.ds(per * TILE, 16), :].astype(F32), axis=0, keepdims=True)
    scale = lax.rsqrt(total / NDST + EPS)
    dest[...] = (share[...] * scale).astype(BF16)
    for i in range(per):
        at = pl.ds(i * TILE, TILE)
        part = own[i] + a[at, :].astype(F32) + b[at, :].astype(F32) + c[at, :].astype(F32)
        caller[at, :] = (part * scale).astype(BF16)


def shifted(value, axis, k, n):
    return lax.ppermute(value, axis, [(i, (i + k) % n) for i in range(n)])


def swap(value):
    return lax.ppermute(value, "layer", [(0, 1), (1, 0)])


def exchange(values, axis, n):
    return [shifted(v, axis, k + 1, n) for k, v in enumerate(values)]


def gather(value, axis, n):
    mine = [value] + [shifted(value, axis, k, n) for k in range(1, n)]
    return mine + [swap(v) for v in mine]


def on_device(tile_values, tile_rows, tile_cols, tile_count, start_panel):
    tiles = tile_values[0, 0, 0]
    rows = tile_rows[0, 0, 0]
    cols = tile_cols[0, 0, 0]
    count = tile_count[0, 0]
    ids = jnp.stack([lax.axis_index(a) for a in ("layer", "x", "col")]).astype(jnp.int32)
    start = start_panel.reshape(DTILES, TILE, RANK)
    quarter = CTILES // 2 // NCOL

    keep, send, tiles = first_pass(rows, cols, count, ids, tiles, start)
    own, *sends = pl.pallas_call(
        first_pair_kernel,
        in_specs=[SMEM, VMEM, VMEM],
        out_specs=[VMEM] * NCOL,
        out_shape=[tiles_of(quarter, F32)] + [tiles_of(quarter, BF16)] * (NCOL - 1),
        compiler_params=PARAMS,
        name="first_pair",
    )(ids, keep, swap(send))
    part = pl.pallas_call(
        caller_kernel,
        in_specs=[VMEM] * NCOL,
        out_specs=VMEM,
        out_shape=tiles_of(quarter, BF16),
        compiler_params=PARAMS,
        name="first_sum",
    )(own, *exchange(sends, "col", NCOL))
    parts = gather(part, "col", NCOL)

    keep, send = tile_pass(back_kernel, cols, rows, count, ids, tiles, parts, DTILES, CTILES, [], "back_pass")
    part = pl.pallas_call(
        back_pair_kernel,
        in_specs=[VMEM, VMEM],
        out_specs=VMEM,
        out_shape=tiles_of(DTILES // 2, BF16),
        compiler_params=PARAMS,
        name="back_pair",
    )(keep, swap(send))
    got = lax.all_to_all(part, ("x", "z"), split_axis=0, concat_axis=0, tiled=True)
    share, copies = pl.pallas_call(
        share_kernel,
        in_specs=[VMEM],
        out_specs=[VMEM, VMEM],
        out_shape=[jax.ShapeDtypeStruct((TILE, RANK), F32), tiles_of(NZ, BF16)],
        compiler_params=PARAMS,
        name="share_sum",
    )(got)
    part = lax.all_to_all(copies, "z", split_axis=0, concat_axis=0, tiled=True)
    parts = gather(part, "x", NX)

    keep, send, squares = tile_pass(
        last_kernel, rows, cols, count, ids, tiles, parts, CTILES, DTILES,
        [jax.ShapeDtypeStruct((8, RANK), F32)], "last_pass",
    )
    chunk = jax.ShapeDtypeStruct((quarter * TILE + 16, RANK), BF16)
    own, *sends = pl.pallas_call(
        last_pair_kernel,
        in_specs=[SMEM, VMEM, VMEM, VMEM],
        out_specs=[VMEM] * NCOL,
        out_shape=[tiles_of(quarter, F32)] + [chunk] * (NCOL - 1),
        compiler_params=PARAMS,
        name="last_pair",
    )(ids, keep, swap(send), squares)
    got = exchange(sends, "col", NCOL)
    caller, dest = pl.pallas_call(
        final_kernel,
        in_specs=[VMEM] * 6,
        out_specs=[VMEM, VMEM],
        out_shape=[
            jax.ShapeDtypeStruct((quarter * TILE, RANK), BF16),
            jax.ShapeDtypeStruct((TILE, RANK), BF16),
        ],
        compiler_params=PARAMS,
        name="final",
    )(own, squares, share, *got)
    return caller[None], dest[None]


def solution(mesh):
    fine = Mesh(mesh.devices.reshape(2, NX, NZ, NCOL), ("layer", "x", "z", "col"))
    row = ("x", "z")
    placed = (
        P("layer", row, "col", None, None, None),
        P("layer", row, "col", None),
        P("layer", row, "col", None),
        P("layer", row, "col"),
        P("col", None),
    )
    return jax.shard_map(
        on_device,
        mesh=fine,
        in_specs=placed,
        out_specs=(P(row, ("layer", "col"), None), P("col", ("layer", "x", "z"), None)),
        check_vma=False,
    )
```

```python
import functools

import jax
import jax.numpy as jnp
from jax import lax
from jax.experimental import pallas as pl
from jax.experimental.pallas import tpu as pltpu
from jax.sharding import Mesh
from jax.sharding import PartitionSpec as P

TILE = 128
RANK = 128
CTILES = 32
DTILES = 64
NX = 4
NZ = 8
NCOL = 4
NDST = 32768
N_SLOTS = 256
SLOT_BITS, ROW_BITS, COL_BITS = 8, 5, 6
BLOCK = 64
UNROLL = 16
EPS = 1e-06

F32 = jnp.float32
BF16 = jnp.bfloat16
CORE, XPOS, COL = 0, 1, 2

SMEM = pl.BlockSpec(memory_space=pltpu.SMEM)
VMEM = pl.BlockSpec(memory_space=pltpu.VMEM)
HBM = pl.BlockSpec(memory_space=pltpu.HBM)
PARAMS = pltpu.CompilerParams(vmem_limit_bytes=40 * 2**20)


def tiles_of(n, dtype):
    return jax.ShapeDtypeStruct((n, TILE, RANK), dtype)


def each(n, body):
    def step(i, carry):
        body(i)
        return carry

    lax.fori_loop(0, n, step, 0)


def accumulate(lo, hi, live, order, tiles, panel, acc, by_row, keep):
    dump = acc.shape[0] - 1

    def group(g, carry):
        for j in range(UNROLL):
            k = g * UNROLL + j
            code = order[N_SLOTS - 1 - k] if keep else order[k]
            row, col = (code >> SLOT_BITS) & (CTILES - 1), code >> (SLOT_BITS + ROW_BITS)
            dst, src = (row, col) if by_row else (col, row)
            tile, block = tiles[code & (N_SLOTS - 1)], panel[src]
            a, b = (tile, block) if by_row else (block, tile)
            acc[jnp.where(k < live, dst & (dump - 1), dump)] += jnp.dot(a, b, preferred_element_type=F32)
        return carry

    lax.fori_loop(lo, hi, group, 0)


def groups(n):
    return (n + UNROLL - 1) // UNROLL


def zero(acc):
    def one(i):
        acc[i] = jnp.zeros((TILE, RANK), F32)

    each(acc.shape[0], one)


def narrow(acc, out):
    def one(i):
        out[i] = acc[i].astype(BF16)

    each(out.shape[0], one)


def sort_slots(first, size, rows, cols, live, core, by_row, by_col, counts):
    def one(i, carry):
        row_sends, row_keeps, col_sends, col_keeps = carry
        t = first + i
        row, col = rows[t], cols[t]
        code = t + (row << SLOT_BITS) + (col << (SLOT_BITS + ROW_BITS))
        used = t < live
        row_own = jnp.where(jnp.logical_and(used, row >> (ROW_BITS - 1) == core), 1, 0)
        col_own = jnp.where(jnp.logical_and(used, col >> (COL_BITS - 1) == core), 1, 0)
        by_row[jnp.where(row_own == 1, N_SLOTS - 1 - row_keeps, row_sends)] = code
        by_col[jnp.where(col_own == 1, N_SLOTS - 1 - col_keeps, col_sends)] = code
        return row_sends + 1 - row_own, row_keeps + row_own, col_sends + 1 - col_own, col_keeps + col_own

    return lax.fori_loop(0, size, one, counts, unroll=4)


def place(ids, parts, panel, axis, n, per):
    core, me = ids[CORE], ids[axis]
    for side in range(2):
        base = jnp.where(side == 0, core, 1 - core) * (n * per)
        for k in range(n):
            at = base + lax.rem(me + n - k, n) * per
            part = parts[side * n + k]

            def one(i):
                panel[at + i] = part[i]

            each(per, one)


def first_send_kernel(
    rows_hbm, cols_hbm, count, ids, tiles_hbm, panel_hbm, send, by_row, by_col, numbers, tiles, panel, rows, cols, acc, sems
):
    lists = [
        pltpu.make_async_copy(rows_hbm, rows, sems.at[0]),
        pltpu.make_async_copy(cols_hbm, cols, sems.at[1]),
    ]
    start = pltpu.make_async_copy(panel_hbm, panel, sems.at[2])
    blocks = [
        pltpu.make_async_copy(
            tiles_hbm.at[pl.ds(i * BLOCK, BLOCK)], tiles.at[pl.ds(i * BLOCK, BLOCK)], sems.at[3 + i]
        )
        for i in range(N_SLOTS // BLOCK)
    ]
    for copy in lists + [start] + blocks:
        copy.start()
    zero(acc)
    for copy in lists:
        copy.wait()
    live, core = count[0], ids[CORE]
    counts, reached = (0, 0, 0, 0), []
    for i in range(N_SLOTS // BLOCK):
        counts = sort_slots(i * BLOCK, BLOCK, rows, cols, live, core, by_row, by_col, counts)
        reached.append(counts[0])
    sends = live - counts[1]
    numbers[0] = sends
    numbers[1] = counts[1]
    numbers[2] = live - counts[3]
    numbers[3] = counts[3]
    start.wait()
    done = 0
    for i in range(N_SLOTS // BLOCK):
        blocks[i].wait()
        ready = jnp.minimum(reached[i], sends)
        until = groups(sends) if i == N_SLOTS // BLOCK - 1 else ready // UNROLL
        accumulate(done, until, sends, by_row, tiles, panel, acc, True, False)
        done = until
    narrow(acc, send)


def in_hbm(value):
    return pltpu.with_memory_space_constraint(value, pltpu.HBM)


def first_send(rows, cols, count, ids, tiles, start):
    n = rows.shape[0]
    words = lambda k: jax.ShapeDtypeStruct((k,), jnp.int32)
    return pl.pallas_call(
        first_send_kernel,
        in_specs=[HBM, HBM, SMEM, SMEM, HBM, HBM],
        out_specs=[VMEM, SMEM, SMEM, SMEM, VMEM, VMEM],
        out_shape=[tiles_of(CTILES // 2, BF16), words(n), words(n), words(4), tiles_of(n, BF16), tiles_of(DTILES, BF16)],
        scratch_shapes=[
            pltpu.SMEM((n,), jnp.int32),
            pltpu.SMEM((n,), jnp.int32),
            pltpu.VMEM((CTILES // 2 + 1, TILE, RANK), F32),
            pltpu.SemaphoreType.DMA((3 + n // BLOCK,)),
        ],
        compiler_params=PARAMS,
        name="first_send",
    )(*(in_hbm(v) for v in (rows, cols)), count, ids, *(in_hbm(v) for v in (tiles, start)))


def send_kernel(order, numbers, ids, tiles, *refs, by_row, axis, n, per):
    parts, (send, panel, acc) = refs[: 2 * n], refs[2 * n :]
    zero(acc)
    place(ids, parts, panel, axis, n, per)
    sends = numbers[0 if by_row else 2]
    accumulate(0, groups(sends), sends, order, tiles, panel, acc, by_row, False)
    narrow(acc, send)


def send_part(order, numbers, ids, tiles, parts, by_row, axis, name):
    n = len(parts) // 2
    per = parts[0].shape[0]
    half = (CTILES if by_row else DTILES) // 2
    return pl.pallas_call(
        functools.partial(send_kernel, by_row=by_row, axis=axis, n=n, per=per),
        in_specs=[SMEM] * 3 + [VMEM] * (1 + len(parts)),
        out_specs=[VMEM, VMEM],
        out_shape=[tiles_of(half, BF16), tiles_of(2 * n * per, BF16)],
        scratch_shapes=[pltpu.VMEM((half + 1, TILE, RANK), F32)],
        compiler_params=PARAMS,
        name=name,
    )(order, numbers, ids, tiles, *parts)


def keep_kernel(order, numbers, tiles, panel, keep, *squares, by_row):
    zero(keep)
    keeps = numbers[1 if by_row else 3]
    accumulate(0, groups(keeps), keeps, order, tiles, panel, keep, by_row, True)
    if squares:

        def one(i, total):
            block = panel[i].astype(F32)
            return total + jnp.sum((block * block).reshape(TILE // 8, 8, RANK), axis=0)

        squares[0][...] = lax.fori_loop(0, DTILES, one, jnp.zeros((8, RANK), F32))


def keep_part(order, numbers, tiles, panel, by_row, extra, name):
    half = (CTILES if by_row else DTILES) // 2
    work = 2 * N_SLOTS * TILE * TILE * RANK
    return pl.pallas_call(
        functools.partial(keep_kernel, by_row=by_row),
        in_specs=[SMEM, SMEM, VMEM, VMEM],
        out_specs=[VMEM] * (1 + len(extra)),
        out_shape=[tiles_of(half + 1, F32)] + extra,
        compiler_params=PARAMS,
        cost_estimate=pl.CostEstimate(flops=work, bytes_accessed=10 * 2**20, transcendentals=0),
        name=name,
    )(order, numbers, tiles, panel)


def pair_kernel(ids, keep, got, own, *sends, axis, n, per):
    me = ids[axis]
    for k in range(n):
        base = lax.rem(me + k, n) * per

        def one(i):
            total = keep[base + i] + got[base + i].astype(F32)
            if k == 0:
                own[i] = total
            else:
                sends[k - 1][i] = total.astype(BF16)

        each(per, one)


def pair_sum(ids, keep, got, axis, n, per, name):
    return pl.pallas_call(
        functools.partial(pair_kernel, axis=axis, n=n, per=per),
        in_specs=[SMEM, VMEM, VMEM],
        out_specs=[VMEM] * n,
        out_shape=[tiles_of(per, F32)] + [tiles_of(per, BF16)] * (n - 1),
        compiler_params=PARAMS,
        name=name,
    )(ids, keep, got)


def caller_kernel(own, a, b, c, out):
    def one(i):
        total = own[i] + a[i].astype(F32) + b[i].astype(F32) + c[i].astype(F32)
        out[i] = total.astype(BF16).astype(F32).T.astype(BF16)

    each(own.shape[0], one)


def row_kernel(own, a, b, c, out):
    def one(i):
        total = own[i] + a[i].astype(F32) + b[i].astype(F32) + c[i].astype(F32)
        out[i] = total.astype(BF16)

    each(own.shape[0], one)


def four_sum(kernel, own, got, name):
    return pl.pallas_call(
        kernel,
        in_specs=[VMEM] * 4,
        out_specs=VMEM,
        out_shape=tiles_of(own.shape[0], BF16),
        compiler_params=PARAMS,
        name=name,
    )(own, *got)


def share_kernel(got, share, copies):
    total = got[0].astype(F32)
    for k in range(1, NZ):
        total += got[k].astype(F32)
    total = total.T
    share[...] = total
    for k in range(NZ):
        copies[k] = total.astype(BF16)


def last_pair_kernel(ids, keep, got, squares, own, *sends):
    me = ids[COL]
    per = CTILES // 2 // NCOL
    total = jnp.sum(squares[...], axis=0, keepdims=True)
    high = total.astype(BF16).astype(F32)
    middle = (total - high).astype(BF16).astype(F32)
    low = total - high - middle
    row = lax.broadcasted_iota(jnp.int32, (16, RANK), 0)
    coded = jnp.where(row == 0, high, jnp.where(row == 1, middle, jnp.where(row == 2, low, 0.0)))
    for k in range(NCOL):
        base = lax.rem(me + k, NCOL) * per
        if k:
            sends[k - 1][pl.ds(per * TILE, 16), :] = coded.astype(BF16)
        for i in range(per):
            part = keep[base + i] + got[base + i].astype(F32)
            if k == 0:
                own[i] = part
            else:
                sends[k - 1][pl.ds(i * TILE, TILE), :] = part.astype(BF16)


def final_kernel(own, squares, share, a, b, c, caller, dest):
    per = CTILES // 2 // NCOL
    total = jnp.sum(squares[...], axis=0, keepdims=True)
    for got in (a, b, c):
        total += jnp.sum(got[pl.ds(per * TILE, 16), :].astype(F32), axis=0, keepdims=True)
    scale = lax.rsqrt(total / NDST + EPS)
    dest[...] = (share[...] * scale).astype(BF16)
    for i in range(per):
        at = pl.ds(i * TILE, TILE)
        part = own[i] + a[at, :].astype(F32) + b[at, :].astype(F32) + c[at, :].astype(F32)
        caller[at, :] = (part * scale).astype(BF16)


def shifted(value, axis, k, n):
    return lax.ppermute(value, axis, [(i, (i + k) % n) for i in range(n)])


def swap(value):
    return lax.ppermute(value, "layer", [(0, 1), (1, 0)])


def exchange(values, axis, n):
    return [shifted(v, axis, k + 1, n) for k, v in enumerate(values)]


def gather(value, axis, n):
    mine = [value] + [shifted(value, axis, k, n) for k in range(1, n)]
    return mine + [swap(v) for v in mine]


def on_device(tile_values, tile_rows, tile_cols, tile_count, start_panel):
    tiles = tile_values[0, 0, 0]
    rows = tile_rows[0, 0, 0]
    cols = tile_cols[0, 0, 0]
    count = tile_count[0, 0]
    ids = jnp.stack([lax.axis_index(a) for a in ("layer", "x", "col")]).astype(jnp.int32)
    start = start_panel.reshape(DTILES, TILE, RANK)
    quarter = CTILES // 2 // NCOL

    send, by_row, by_col, numbers, tiles, panel = first_send(rows, cols, count, ids, tiles, start)
    got = swap(send)
    [keep] = keep_part(by_row, numbers, tiles, panel, True, [], "first_keep")
    own, *sends = pair_sum(ids, keep, got, COL, NCOL, quarter, "first_pair")
    part = four_sum(caller_kernel, own, exchange(sends, "col", NCOL), "first_sum")
    parts = gather(part, "col", NCOL)

    send, panel = send_part(by_col, numbers, ids, tiles, parts, False, COL, "back_send")
    got = swap(send)
    [keep] = keep_part(by_col, numbers, tiles, panel, False, [], "back_keep")
    own, *sends = pair_sum(ids, keep, got, XPOS, NX, NZ, "back_pair")
    part = four_sum(row_kernel, own, exchange(sends, "x", NX), "back_sum")
    got = lax.all_to_all(part, "z", split_axis=0, concat_axis=0, tiled=True)
    share, copies = pl.pallas_call(
        share_kernel,
        in_specs=[VMEM],
        out_specs=[VMEM, VMEM],
        out_shape=[jax.ShapeDtypeStruct((TILE, RANK), F32), tiles_of(NZ, BF16)],
        compiler_params=PARAMS,
        name="share_sum",
    )(got)
    part = lax.all_to_all(copies, "z", split_axis=0, concat_axis=0, tiled=True)
    parts = gather(part, "x", NX)

    send, panel = send_part(by_row, numbers, ids, tiles, parts, True, XPOS, "last_send")
    got = swap(send)
    keep, squares = keep_part(
        by_row, numbers, tiles, panel, True, [jax.ShapeDtypeStruct((8, RANK), F32)], "last_keep"
    )
    chunk = jax.ShapeDtypeStruct((quarter * TILE + 16, RANK), BF16)
    own, *sends = pl.pallas_call(
        last_pair_kernel,
        in_specs=[SMEM, VMEM, VMEM, VMEM],
        out_specs=[VMEM] * NCOL,
        out_shape=[tiles_of(quarter, F32)] + [chunk] * (NCOL - 1),
        compiler_params=PARAMS,
        name="last_pair",
    )(ids, keep, got, squares)
    got = exchange(sends, "col", NCOL)
    caller, dest = pl.pallas_call(
        final_kernel,
        in_specs=[VMEM] * 6,
        out_specs=[VMEM, VMEM],
        out_shape=[
            jax.ShapeDtypeStruct((quarter * TILE, RANK), BF16),
            jax.ShapeDtypeStruct((TILE, RANK), BF16),
        ],
        compiler_params=PARAMS,
        name="final",
    )(own, squares, share, *got)
    return caller[None], dest[None]


def solution(mesh):
    fine = Mesh(mesh.devices.reshape(2, NX, NZ, NCOL), ("layer", "x", "z", "col"))
    row = ("x", "z")
    placed = (
        P("layer", row, "col", None, None, None),
        P("layer", row, "col", None),
        P("layer", row, "col", None),
        P("layer", row, "col"),
        P("col", None),
    )
    return jax.shard_map(
        on_device,
        mesh=fine,
        in_specs=placed,
        out_specs=(P(row, ("layer", "col"), None), P("col", ("layer", "x", "z"), None)),
        check_vma=False,
    )
```

```python
import functools

import jax
import jax.numpy as jnp
from jax import lax
from jax.experimental import pallas as pl
from jax.experimental.pallas import tpu as pltpu
from jax.sharding import Mesh
from jax.sharding import PartitionSpec as P

TILE = 128
RANK = 128
CTILES = 32
DTILES = 64
NX = 4
NZ = 8
NCOL = 4
NDST = 32768
N_SLOTS = 256
SLOT_BITS, ROW_BITS, COL_BITS = 8, 5, 6
BLOCK = 64
UNROLL = 16
STEPS = 4
EPS = 1e-06

F32 = jnp.float32
BF16 = jnp.bfloat16
CORE, XPOS, COL = 0, 1, 2

SMEM = pl.BlockSpec(memory_space=pltpu.SMEM)
VMEM = pl.BlockSpec(memory_space=pltpu.VMEM)
HBM = pl.BlockSpec(memory_space=pltpu.HBM)
PARAMS = pltpu.CompilerParams(vmem_limit_bytes=40 * 2**20)


def tiles_of(n, dtype):
    return jax.ShapeDtypeStruct((n, TILE, RANK), dtype)


def each(n, body):
    whole = n // STEPS

    def step(i, carry):
        for j in range(STEPS):
            body(i * STEPS + j)
        return carry

    if whole > 1:
        lax.fori_loop(0, whole, step, 0)
    for i in range(whole * STEPS if whole > 1 else 0, n):
        body(i)


def accumulate(lo, hi, live, order, tiles, panel, acc, by_row, keep):
    dump = acc.shape[0] - 1

    def group(g, carry):
        for j in range(UNROLL):
            k = g * UNROLL + j
            code = order[N_SLOTS - 1 - k] if keep else order[k]
            row, col = (code >> SLOT_BITS) & (CTILES - 1), code >> (SLOT_BITS + ROW_BITS)
            dst, src = (row, col) if by_row else (col, row)
            tile, block = tiles[code & (N_SLOTS - 1)], panel[src]
            a, b = (tile, block) if by_row else (block, tile)
            acc[jnp.where(k < live, dst & (dump - 1), dump)] += jnp.dot(a, b, preferred_element_type=F32)
        return carry

    lax.fori_loop(lo, hi, group, 0)


def groups(n):
    return (n + UNROLL - 1) // UNROLL


def zero(acc):
    def one(i):
        acc[i] = jnp.zeros((TILE, RANK), F32)

    each(acc.shape[0], one)


def narrow(acc, out):
    def one(i):
        out[i] = acc[i].astype(BF16)

    each(out.shape[0], one)


def sort_slots(first, size, rows, cols, live, core, by_row, by_col, counts):
    def one(i, carry):
        row_sends, row_keeps, col_sends, col_keeps = carry
        t = first + i
        row, col = rows[t], cols[t]
        code = t + (row << SLOT_BITS) + (col << (SLOT_BITS + ROW_BITS))
        used = t < live
        row_own = jnp.where(jnp.logical_and(used, row >> (ROW_BITS - 1) == core), 1, 0)
        col_own = jnp.where(jnp.logical_and(used, col >> (COL_BITS - 1) == core), 1, 0)
        by_row[jnp.where(row_own == 1, N_SLOTS - 1 - row_keeps, row_sends)] = code
        by_col[jnp.where(col_own == 1, N_SLOTS - 1 - col_keeps, col_sends)] = code
        return row_sends + 1 - row_own, row_keeps + row_own, col_sends + 1 - col_own, col_keeps + col_own

    return lax.fori_loop(0, size, one, counts, unroll=4)


def place(ids, parts, panel, axis, n, per):
    core, me = ids[CORE], ids[axis]
    for side in range(2):
        base = jnp.where(side == 0, core, 1 - core) * (n * per)
        for k in range(n):
            at = base + lax.rem(me + n - k, n) * per
            part = parts[side * n + k]

            def one(i):
                panel[at + i] = part[i]

            each(per, one)


def first_send_kernel(
    rows_hbm, cols_hbm, count, ids, tiles_hbm, panel_hbm, send, by_row, by_col, numbers, tiles, panel, rows, cols, acc, sems
):
    lists = [
        pltpu.make_async_copy(rows_hbm, rows, sems.at[0]),
        pltpu.make_async_copy(cols_hbm, cols, sems.at[1]),
    ]
    start = pltpu.make_async_copy(panel_hbm, panel, sems.at[2])
    blocks = [
        pltpu.make_async_copy(
            tiles_hbm.at[pl.ds(i * BLOCK, BLOCK)], tiles.at[pl.ds(i * BLOCK, BLOCK)], sems.at[3 + i]
        )
        for i in range(N_SLOTS // BLOCK)
    ]
    for copy in lists + [start] + blocks:
        copy.start()
    zero(acc)
    for copy in lists:
        copy.wait()
    live, core = count[0], ids[CORE]
    counts, done, last = (0, 0, 0, 0), 0, N_SLOTS // BLOCK - 1
    for i in range(last + 1):
        counts = sort_slots(i * BLOCK, BLOCK, rows, cols, live, core, by_row, by_col, counts)
        sends = jnp.minimum(live, (i + 1) * BLOCK) - counts[1]
        if i == 0:
            start.wait()
        blocks[i].wait()
        until = groups(sends) if i == last else sends // UNROLL
        accumulate(done, until, sends, by_row, tiles, panel, acc, True, False)
        done = until
    numbers[0] = live - counts[1]
    numbers[1] = counts[1]
    numbers[2] = live - counts[3]
    numbers[3] = counts[3]
    narrow(acc, send)


def in_hbm(value):
    return pltpu.with_memory_space_constraint(value, pltpu.HBM)


def first_send(rows, cols, count, ids, tiles, start):
    n = rows.shape[0]
    words = lambda k: jax.ShapeDtypeStruct((k,), jnp.int32)
    return pl.pallas_call(
        first_send_kernel,
        in_specs=[HBM, HBM, SMEM, SMEM, HBM, HBM],
        out_specs=[VMEM, SMEM, SMEM, SMEM, VMEM, VMEM],
        out_shape=[tiles_of(CTILES // 2, BF16), words(n), words(n), words(4), tiles_of(n, BF16), tiles_of(DTILES, BF16)],
        scratch_shapes=[
            pltpu.SMEM((n,), jnp.int32),
            pltpu.SMEM((n,), jnp.int32),
            pltpu.VMEM((CTILES // 2 + 1, TILE, RANK), F32),
            pltpu.SemaphoreType.DMA((3 + n // BLOCK,)),
        ],
        compiler_params=PARAMS,
        name="first_send",
    )(*(in_hbm(v) for v in (rows, cols)), count, ids, *(in_hbm(v) for v in (tiles, start)))


def send_kernel(order, numbers, ids, tiles, *refs, by_row, axis, n, per):
    parts, (send, panel, acc) = refs[: 2 * n], refs[2 * n :]
    zero(acc)
    place(ids, parts, panel, axis, n, per)
    sends = numbers[0 if by_row else 2]
    accumulate(0, groups(sends), sends, order, tiles, panel, acc, by_row, False)
    narrow(acc, send)


def send_part(order, numbers, ids, tiles, parts, by_row, axis, name):
    n = len(parts) // 2
    per = parts[0].shape[0]
    half = (CTILES if by_row else DTILES) // 2
    return pl.pallas_call(
        functools.partial(send_kernel, by_row=by_row, axis=axis, n=n, per=per),
        in_specs=[SMEM] * 3 + [VMEM] * (1 + len(parts)),
        out_specs=[VMEM, VMEM],
        out_shape=[tiles_of(half, BF16), tiles_of(2 * n * per, BF16)],
        scratch_shapes=[pltpu.VMEM((half + 1, TILE, RANK), F32)],
        compiler_params=PARAMS,
        name=name,
    )(order, numbers, ids, tiles, *parts)


def keep_kernel(order, numbers, tiles, panel, keep, *squares, by_row):
    zero(keep)
    keeps = numbers[1 if by_row else 3]
    accumulate(0, groups(keeps), keeps, order, tiles, panel, keep, by_row, True)
    if squares:

        def one(i, total):
            block = panel[i].astype(F32)
            return total + jnp.sum((block * block).reshape(4, TILE // 4, RANK), axis=0)

        squares[0][...] = lax.fori_loop(0, DTILES, one, jnp.zeros((TILE // 4, RANK), F32))


def keep_part(order, numbers, tiles, panel, by_row, extra, name):
    half = (CTILES if by_row else DTILES) // 2
    work = 2 * N_SLOTS * TILE * TILE * RANK
    return pl.pallas_call(
        functools.partial(keep_kernel, by_row=by_row),
        in_specs=[SMEM, SMEM, VMEM, VMEM],
        out_specs=[VMEM] * (1 + len(extra)),
        out_shape=[tiles_of(half + 1, F32)] + extra,
        compiler_params=PARAMS,
        cost_estimate=pl.CostEstimate(flops=work, bytes_accessed=10 * 2**20, transcendentals=0),
        name=name,
    )(order, numbers, tiles, panel)


def pair_kernel(ids, keep, got, own, *sends, axis, n, per):
    me = ids[axis]
    for k in range(n):
        base = lax.rem(me + k, n) * per

        def one(i):
            total = keep[base + i] + got[base + i].astype(F32)
            if k == 0:
                own[i] = total
            else:
                sends[k - 1][i] = total.astype(BF16)

        each(per, one)


def pair_sum(ids, keep, got, axis, n, per, name):
    return pl.pallas_call(
        functools.partial(pair_kernel, axis=axis, n=n, per=per),
        in_specs=[SMEM, VMEM, VMEM],
        out_specs=[VMEM] * n,
        out_shape=[tiles_of(per, F32)] + [tiles_of(per, BF16)] * (n - 1),
        compiler_params=PARAMS,
        name=name,
    )(ids, keep, got)


def caller_kernel(own, a, b, c, out):
    def one(i):
        total = own[i] + a[i].astype(F32) + b[i].astype(F32) + c[i].astype(F32)
        out[i] = total.astype(BF16).astype(F32).T.astype(BF16)

    each(own.shape[0], one)


def row_kernel(own, a, b, c, out):
    def one(i):
        total = own[i] + a[i].astype(F32) + b[i].astype(F32) + c[i].astype(F32)
        out[i] = total.astype(BF16)

    each(own.shape[0], one)


def four_sum(kernel, own, got, name):
    return pl.pallas_call(
        kernel,
        in_specs=[VMEM] * 4,
        out_specs=VMEM,
        out_shape=tiles_of(own.shape[0], BF16),
        compiler_params=PARAMS,
        name=name,
    )(own, *got)


def share_kernel(got, share, copies):
    total = got[0].astype(F32)
    for k in range(1, NZ):
        total += got[k].astype(F32)
    total = total.T
    share[...] = total
    for k in range(NZ):
        copies[k] = total.astype(BF16)


def last_pair_kernel(ids, keep, got, squares, own, *sends):
    me = ids[COL]
    per = CTILES // 2 // NCOL
    total = jnp.sum(squares[...], axis=0, keepdims=True)
    high = total.astype(BF16).astype(F32)
    middle = (total - high).astype(BF16).astype(F32)
    low = total - high - middle
    row = lax.broadcasted_iota(jnp.int32, (16, RANK), 0)
    coded = jnp.where(row == 0, high, jnp.where(row == 1, middle, jnp.where(row == 2, low, 0.0)))
    for k in range(NCOL):
        base = lax.rem(me + k, NCOL) * per
        if k:
            sends[k - 1][pl.ds(per * TILE, 16), :] = coded.astype(BF16)
        for i in range(per):
            part = keep[base + i] + got[base + i].astype(F32)
            if k == 0:
                own[i] = part
            else:
                sends[k - 1][pl.ds(i * TILE, TILE), :] = part.astype(BF16)


def final_kernel(own, squares, share, a, b, c, caller, dest):
    per = CTILES // 2 // NCOL
    total = jnp.sum(squares[...], axis=0, keepdims=True)
    for got in (a, b, c):
        total += jnp.sum(got[pl.ds(per * TILE, 16), :].astype(F32), axis=0, keepdims=True)
    scale = lax.rsqrt(total / NDST + EPS)
    dest[...] = (share[...] * scale).astype(BF16)
    for i in range(per):
        at = pl.ds(i * TILE, TILE)
        part = own[i] + a[at, :].astype(F32) + b[at, :].astype(F32) + c[at, :].astype(F32)
        caller[at, :] = (part * scale).astype(BF16)


def shifted(value, axis, k, n):
    return lax.ppermute(value, axis, [(i, (i + k) % n) for i in range(n)])


def swap(value):
    return lax.ppermute(value, "layer", [(0, 1), (1, 0)])


def exchange(values, axis, n):
    return [shifted(v, axis, k + 1, n) for k, v in enumerate(values)]


def gather(value, axis, n):
    mine = [value] + [shifted(value, axis, k, n) for k in range(1, n)]
    return mine + [swap(v) for v in mine]


def on_device(tile_values, tile_rows, tile_cols, tile_count, start_panel):
    tiles = tile_values[0, 0, 0]
    rows = tile_rows[0, 0, 0]
    cols = tile_cols[0, 0, 0]
    count = tile_count[0, 0]
    ids = jnp.stack([lax.axis_index(a) for a in ("layer", "x", "col")]).astype(jnp.int32)
    start = start_panel.reshape(DTILES, TILE, RANK)
    quarter = CTILES // 2 // NCOL

    send, by_row, by_col, numbers, tiles, panel = first_send(rows, cols, count, ids, tiles, start)
    got = swap(send)
    [keep] = keep_part(by_row, numbers, tiles, panel, True, [], "first_keep")
    own, *sends = pair_sum(ids, keep, got, COL, NCOL, quarter, "first_pair")
    part = four_sum(caller_kernel, own, exchange(sends, "col", NCOL), "first_sum")
    parts = gather(part, "col", NCOL)

    send, panel = send_part(by_col, numbers, ids, tiles, parts, False, COL, "back_send")
    got = swap(send)
    [keep] = keep_part(by_col, numbers, tiles, panel, False, [], "back_keep")
    own, *sends = pair_sum(ids, keep, got, XPOS, NX, NZ, "back_pair")
    part = four_sum(row_kernel, own, exchange(sends, "x", NX), "back_sum")
    got = lax.all_to_all(part, "z", split_axis=0, concat_axis=0, tiled=True)
    share, copies = pl.pallas_call(
        share_kernel,
        in_specs=[VMEM],
        out_specs=[VMEM, VMEM],
        out_shape=[jax.ShapeDtypeStruct((TILE, RANK), F32), tiles_of(NZ, BF16)],
        compiler_params=PARAMS,
        name="share_sum",
    )(got)
    part = lax.all_to_all(copies, "z", split_axis=0, concat_axis=0, tiled=True)
    parts = gather(part, "x", NX)

    send, panel = send_part(by_row, numbers, ids, tiles, parts, True, XPOS, "last_send")
    got = swap(send)
    keep, squares = keep_part(
        by_row, numbers, tiles, panel, True, [jax.ShapeDtypeStruct((TILE // 4, RANK), F32)], "last_keep"
    )
    chunk = jax.ShapeDtypeStruct((quarter * TILE + 16, RANK), BF16)
    own, *sends = pl.pallas_call(
        last_pair_kernel,
        in_specs=[SMEM, VMEM, VMEM, VMEM],
        out_specs=[VMEM] * NCOL,
        out_shape=[tiles_of(quarter, F32)] + [chunk] * (NCOL - 1),
        compiler_params=PARAMS,
        name="last_pair",
    )(ids, keep, got, squares)
    got = exchange(sends, "col", NCOL)
    caller, dest = pl.pallas_call(
        final_kernel,
        in_specs=[VMEM] * 6,
        out_specs=[VMEM, VMEM],
        out_shape=[
            jax.ShapeDtypeStruct((quarter * TILE, RANK), BF16),
            jax.ShapeDtypeStruct((TILE, RANK), BF16),
        ],
        compiler_params=PARAMS,
        name="final",
    )(own, squares, share, *got)
    return caller[None], dest[None]


def solution(mesh):
    fine = Mesh(mesh.devices.reshape(2, NX, NZ, NCOL), ("layer", "x", "z", "col"))
    row = ("x", "z")
    placed = (
        P("layer", row, "col", None, None, None),
        P("layer", row, "col", None),
        P("layer", row, "col", None),
        P("layer", row, "col"),
        P("col", None),
    )
    return jax.shard_map(
        on_device,
        mesh=fine,
        in_specs=placed,
        out_specs=(P(row, ("layer", "col"), None), P("col", ("layer", "x", "z"), None)),
        check_vma=False,
    )
```

```python
import functools

import jax
import jax.numpy as jnp
from jax import lax
from jax.experimental import pallas as pl
from jax.experimental.pallas import tpu as pltpu
from jax.sharding import Mesh
from jax.sharding import PartitionSpec as P

TILE = 128
RANK = 128
CTILES = 32
DTILES = 64
NX = 4
NZ = 8
NCOL = 4
NDST = 32768
N_SLOTS = 256
SLOT_BITS, ROW_BITS, COL_BITS = 8, 5, 6
BLOCK = 64
UNROLL = 16
STEPS = 4
SORT_STEP = 16
SHIFTS = (0, 2, 1, 3)
GATHER_SHIFTS = (0, 1, 3, 2)
EPS = 1e-06

F32 = jnp.float32
BF16 = jnp.bfloat16
CORE, XPOS, COL = 0, 1, 2

SMEM = pl.BlockSpec(memory_space=pltpu.SMEM)
VMEM = pl.BlockSpec(memory_space=pltpu.VMEM)
HBM = pl.BlockSpec(memory_space=pltpu.HBM)
PARAMS = pltpu.CompilerParams(vmem_limit_bytes=40 * 2**20)


def tiles_of(n, dtype):
    return jax.ShapeDtypeStruct((n, TILE, RANK), dtype)


def each(n, body):
    whole = n // STEPS

    def step(i, carry):
        for j in range(STEPS):
            body(i * STEPS + j)
        return carry

    if whole > 1:
        lax.fori_loop(0, whole, step, 0)
    for i in range(whole * STEPS if whole > 1 else 0, n):
        body(i)


def accumulate(lo, hi, live, order, tiles, panel, acc, by_row, keep):
    dump = acc.shape[0] - 1

    def group(g, carry):
        for j in range(UNROLL):
            k = g * UNROLL + j
            code = order[N_SLOTS - 1 - k] if keep else order[k]
            row, col = (code >> SLOT_BITS) & (CTILES - 1), code >> (SLOT_BITS + ROW_BITS)
            dst, src = (row, col) if by_row else (col, row)
            tile, block = tiles[code & (N_SLOTS - 1)], panel[src]
            a, b = (tile, block) if by_row else (block, tile)
            acc[jnp.where(k < live, dst & (dump - 1), dump)] += jnp.dot(a, b, preferred_element_type=F32)
        return carry

    lax.fori_loop(lo, hi, group, 0)


def groups(n):
    return (n + UNROLL - 1) // UNROLL


def zero(acc):
    def one(i):
        acc[i] = jnp.zeros((TILE, RANK), F32)

    each(acc.shape[0], one)


def narrow(acc, out):
    def one(i):
        out[i] = acc[i].astype(BF16)

    each(out.shape[0], one)


def sort_slots(first, size, rows, cols, live, core, by_row, by_col, counts):
    def several(g, carry):
        row_sends, row_keeps, col_sends, col_keeps = carry
        slots = [first + g * SORT_STEP + j for j in range(SORT_STEP)]
        loaded = [(t, rows[t], cols[t]) for t in slots]
        for t, row, col in loaded:
            code = t + (row << SLOT_BITS) + (col << (SLOT_BITS + ROW_BITS))
            used = t < live
            row_own = jnp.where(jnp.logical_and(used, row >> (ROW_BITS - 1) == core), 1, 0)
            col_own = jnp.where(jnp.logical_and(used, col >> (COL_BITS - 1) == core), 1, 0)
            by_row[jnp.where(row_own == 1, N_SLOTS - 1 - row_keeps, row_sends)] = code
            by_col[jnp.where(col_own == 1, N_SLOTS - 1 - col_keeps, col_sends)] = code
            row_sends, row_keeps = row_sends + 1 - row_own, row_keeps + row_own
            col_sends, col_keeps = col_sends + 1 - col_own, col_keeps + col_own
        return row_sends, row_keeps, col_sends, col_keeps

    return lax.fori_loop(0, size // SORT_STEP, several, counts)


def place(ids, parts, panel, axis, n, per):
    core, me = ids[CORE], ids[axis]
    for side in range(2):
        base = jnp.where(side == 0, core, 1 - core) * (n * per)
        for k in range(n):
            at = base + lax.rem(me + n - GATHER_SHIFTS[k], n) * per
            part = parts[side * n + k]

            def one(i):
                panel[at + i] = part[i]

            each(per, one)


def first_send_kernel(
    rows_hbm, cols_hbm, count, ids, tiles_hbm, panel_hbm, send, by_row, by_col, numbers, tiles, panel, rows, cols, acc, sems
):
    lists = [
        pltpu.make_async_copy(rows_hbm, rows, sems.at[0]),
        pltpu.make_async_copy(cols_hbm, cols, sems.at[1]),
    ]
    start = pltpu.make_async_copy(panel_hbm, panel, sems.at[2])
    blocks = [
        pltpu.make_async_copy(
            tiles_hbm.at[pl.ds(i * BLOCK, BLOCK)], tiles.at[pl.ds(i * BLOCK, BLOCK)], sems.at[3 + i]
        )
        for i in range(N_SLOTS // BLOCK)
    ]
    for copy in lists + [start] + blocks:
        copy.start()
    zero(acc)
    for copy in lists:
        copy.wait()
    live, core = count[0], ids[CORE]
    counts, done, last = (0, 0, 0, 0), 0, N_SLOTS // BLOCK - 1
    for i in range(last + 1):
        counts = sort_slots(i * BLOCK, BLOCK, rows, cols, live, core, by_row, by_col, counts)
        sends = jnp.minimum(live, (i + 1) * BLOCK) - counts[1]
        if i == 0:
            start.wait()
        blocks[i].wait()
        until = groups(sends) if i == last else sends // UNROLL
        accumulate(done, until, sends, by_row, tiles, panel, acc, True, False)
        done = until
    numbers[0] = live - counts[1]
    numbers[1] = counts[1]
    numbers[2] = live - counts[3]
    numbers[3] = counts[3]
    narrow(acc, send)


def in_hbm(value):
    return pltpu.with_memory_space_constraint(value, pltpu.HBM)


def first_send(rows, cols, count, ids, tiles, start):
    n = rows.shape[0]
    words = lambda k: jax.ShapeDtypeStruct((k,), jnp.int32)
    return pl.pallas_call(
        first_send_kernel,
        in_specs=[HBM, HBM, SMEM, SMEM, HBM, HBM],
        out_specs=[VMEM, SMEM, SMEM, SMEM, VMEM, VMEM],
        out_shape=[tiles_of(CTILES // 2, BF16), words(n), words(n), words(4), tiles_of(n, BF16), tiles_of(DTILES, BF16)],
        scratch_shapes=[
            pltpu.SMEM((n,), jnp.int32),
            pltpu.SMEM((n,), jnp.int32),
            pltpu.VMEM((CTILES // 2 + 1, TILE, RANK), F32),
            pltpu.SemaphoreType.DMA((3 + n // BLOCK,)),
        ],
        compiler_params=PARAMS,
        name="first_send",
    )(*(in_hbm(v) for v in (rows, cols)), count, ids, *(in_hbm(v) for v in (tiles, start)))


def send_kernel(order, numbers, ids, tiles, *refs, by_row, axis, n, per):
    parts, (send, panel, acc) = refs[: 2 * n], refs[2 * n :]
    zero(acc)
    place(ids, parts, panel, axis, n, per)
    sends = numbers[0 if by_row else 2]
    accumulate(0, groups(sends), sends, order, tiles, panel, acc, by_row, False)
    narrow(acc, send)


def send_part(order, numbers, ids, tiles, parts, by_row, axis, name):
    n = len(parts) // 2
    per = parts[0].shape[0]
    half = (CTILES if by_row else DTILES) // 2
    return pl.pallas_call(
        functools.partial(send_kernel, by_row=by_row, axis=axis, n=n, per=per),
        in_specs=[SMEM] * 3 + [VMEM] * (1 + len(parts)),
        out_specs=[VMEM, VMEM],
        out_shape=[tiles_of(half, BF16), tiles_of(2 * n * per, BF16)],
        scratch_shapes=[pltpu.VMEM((half + 1, TILE, RANK), F32)],
        compiler_params=PARAMS,
        name=name,
    )(order, numbers, ids, tiles, *parts)


def keep_kernel(order, numbers, tiles, panel, keep, *squares, by_row):
    zero(keep)
    keeps = numbers[1 if by_row else 3]
    accumulate(0, groups(keeps), keeps, order, tiles, panel, keep, by_row, True)
    if squares:

        def one(i, total):
            block = panel[i].astype(F32)
            return total + jnp.sum((block * block).reshape(4, TILE // 4, RANK), axis=0)

        squares[0][...] = lax.fori_loop(0, DTILES, one, jnp.zeros((TILE // 4, RANK), F32))


def keep_part(order, numbers, tiles, panel, by_row, extra, name):
    half = (CTILES if by_row else DTILES) // 2
    work = 2 * N_SLOTS * TILE * TILE * RANK
    return pl.pallas_call(
        functools.partial(keep_kernel, by_row=by_row),
        in_specs=[SMEM, SMEM, VMEM, VMEM],
        out_specs=[VMEM] * (1 + len(extra)),
        out_shape=[tiles_of(half + 1, F32)] + extra,
        compiler_params=PARAMS,
        cost_estimate=pl.CostEstimate(flops=work, bytes_accessed=10 * 2**20, transcendentals=0),
        name=name,
    )(order, numbers, tiles, panel)


def pair_kernel(ids, keep, got, own, *sends, axis, n, per):
    me = ids[axis]
    for k in range(n):
        base = lax.rem(me + SHIFTS[k], n) * per

        def one(i):
            total = keep[base + i] + got[base + i].astype(F32)
            if k == 0:
                own[i] = total
            else:
                sends[k - 1][i] = total.astype(BF16)

        each(per, one)


def pair_sum(ids, keep, got, axis, n, per, name):
    return pl.pallas_call(
        functools.partial(pair_kernel, axis=axis, n=n, per=per),
        in_specs=[SMEM, VMEM, VMEM],
        out_specs=[VMEM] * n,
        out_shape=[tiles_of(per, F32)] + [tiles_of(per, BF16)] * (n - 1),
        compiler_params=PARAMS,
        name=name,
    )(ids, keep, got)


def caller_kernel(own, a, b, c, out):
    def one(i):
        total = own[i] + a[i].astype(F32) + b[i].astype(F32) + c[i].astype(F32)
        out[i] = total.astype(BF16).astype(F32).T.astype(BF16)

    each(own.shape[0], one)


def row_kernel(own, a, b, c, out):
    def one(i):
        total = own[i] + a[i].astype(F32) + b[i].astype(F32) + c[i].astype(F32)
        out[i] = total.astype(BF16)

    each(own.shape[0], one)


def four_sum(kernel, own, got, name):
    return pl.pallas_call(
        kernel,
        in_specs=[VMEM] * 4,
        out_specs=VMEM,
        out_shape=tiles_of(own.shape[0], BF16),
        compiler_params=PARAMS,
        name=name,
    )(own, *got)


def share_kernel(got, share, copies):
    total = got[0].astype(F32)
    for k in range(1, NZ):
        total += got[k].astype(F32)
    total = total.T
    share[...] = total
    for k in range(NZ):
        copies[k] = total.astype(BF16)


def last_pair_kernel(ids, keep, got, squares, own, *sends):
    me = ids[COL]
    per = CTILES // 2 // NCOL
    total = jnp.sum(squares[...], axis=0, keepdims=True)
    high = total.astype(BF16).astype(F32)
    middle = (total - high).astype(BF16).astype(F32)
    low = total - high - middle
    row = lax.broadcasted_iota(jnp.int32, (16, RANK), 0)
    coded = jnp.where(row == 0, high, jnp.where(row == 1, middle, jnp.where(row == 2, low, 0.0)))
    for k in range(NCOL):
        base = lax.rem(me + SHIFTS[k], NCOL) * per
        if k:
            sends[k - 1][pl.ds(per * TILE, 16), :] = coded.astype(BF16)
        for i in range(per):
            part = keep[base + i] + got[base + i].astype(F32)
            if k == 0:
                own[i] = part
            else:
                sends[k - 1][pl.ds(i * TILE, TILE), :] = part.astype(BF16)


def final_kernel(own, squares, share, a, b, c, caller, dest):
    per = CTILES // 2 // NCOL
    total = jnp.sum(squares[...], axis=0, keepdims=True)
    for got in (a, b, c):
        total += jnp.sum(got[pl.ds(per * TILE, 16), :].astype(F32), axis=0, keepdims=True)
    scale = lax.rsqrt(total / NDST + EPS)
    dest[...] = (share[...] * scale).astype(BF16)
    for i in range(per):
        at = pl.ds(i * TILE, TILE)
        part = own[i] + a[at, :].astype(F32) + b[at, :].astype(F32) + c[at, :].astype(F32)
        caller[at, :] = (part * scale).astype(BF16)


def shifted(value, axis, k, n):
    return lax.ppermute(value, axis, [(i, (i + k) % n) for i in range(n)])


def swap(value):
    return lax.ppermute(value, "layer", [(0, 1), (1, 0)])


def exchange(values, axis, n):
    return [shifted(v, axis, k, n) for v, k in zip(values, SHIFTS[1:], strict=True)]


def gather(value, axis, n):
    mine = [value] + [shifted(value, axis, k, n) for k in GATHER_SHIFTS[1:]]
    return mine + [swap(v) for v in mine]


def on_device(tile_values, tile_rows, tile_cols, tile_count, start_panel):
    tiles = tile_values[0, 0, 0]
    rows = tile_rows[0, 0, 0]
    cols = tile_cols[0, 0, 0]
    count = tile_count[0, 0]
    ids = jnp.stack([lax.axis_index(a) for a in ("layer", "x", "col")]).astype(jnp.int32)
    start = start_panel.reshape(DTILES, TILE, RANK)
    quarter = CTILES // 2 // NCOL

    send, by_row, by_col, numbers, tiles, panel = first_send(rows, cols, count, ids, tiles, start)
    got = swap(send)
    [keep] = keep_part(by_row, numbers, tiles, panel, True, [], "first_keep")
    own, *sends = pair_sum(ids, keep, got, COL, NCOL, quarter, "first_pair")
    part = four_sum(caller_kernel, own, exchange(sends, "col", NCOL), "first_sum")
    parts = gather(part, "col", NCOL)

    send, panel = send_part(by_col, numbers, ids, tiles, parts, False, COL, "back_send")
    got = swap(send)
    [keep] = keep_part(by_col, numbers, tiles, panel, False, [], "back_keep")
    own, *sends = pair_sum(ids, keep, got, XPOS, NX, NZ, "back_pair")
    part = four_sum(row_kernel, own, exchange(sends, "x", NX), "back_sum")
    got = lax.all_to_all(part, "z", split_axis=0, concat_axis=0, tiled=True)
    share, copies = pl.pallas_call(
        share_kernel,
        in_specs=[VMEM],
        out_specs=[VMEM, VMEM],
        out_shape=[jax.ShapeDtypeStruct((TILE, RANK), F32), tiles_of(NZ, BF16)],
        compiler_params=PARAMS,
        name="share_sum",
    )(got)
    part = lax.all_to_all(copies, "z", split_axis=0, concat_axis=0, tiled=True)
    parts = gather(part, "x", NX)

    send, panel = send_part(by_row, numbers, ids, tiles, parts, True, XPOS, "last_send")
    got = swap(send)
    keep, squares = keep_part(
        by_row, numbers, tiles, panel, True, [jax.ShapeDtypeStruct((TILE // 4, RANK), F32)], "last_keep"
    )
    chunk = jax.ShapeDtypeStruct((quarter * TILE + 16, RANK), BF16)
    own, *sends = pl.pallas_call(
        last_pair_kernel,
        in_specs=[SMEM, VMEM, VMEM, VMEM],
        out_specs=[VMEM] * NCOL,
        out_shape=[tiles_of(quarter, F32)] + [chunk] * (NCOL - 1),
        compiler_params=PARAMS,
        name="last_pair",
    )(ids, keep, got, squares)
    got = exchange(sends, "col", NCOL)
    caller, dest = pl.pallas_call(
        final_kernel,
        in_specs=[VMEM] * 6,
        out_specs=[VMEM, VMEM],
        out_shape=[
            jax.ShapeDtypeStruct((quarter * TILE, RANK), BF16),
            jax.ShapeDtypeStruct((TILE, RANK), BF16),
        ],
        compiler_params=PARAMS,
        name="final",
    )(own, squares, share, *got)
    return caller[None], dest[None]


def solution(mesh):
    fine = Mesh(mesh.devices.reshape(2, NX, NZ, NCOL), ("layer", "x", "z", "col"))
    row = ("x", "z")
    placed = (
        P("layer", row, "col", None, None, None),
        P("layer", row, "col", None),
        P("layer", row, "col", None),
        P("layer", row, "col"),
        P("col", None),
    )
    return jax.shard_map(
        on_device,
        mesh=fine,
        in_specs=placed,
        out_specs=(P(row, ("layer", "col"), None), P("col", ("layer", "x", "z"), None)),
        check_vma=False,
    )
```

```python
import functools

import jax
import jax.numpy as jnp
from jax import lax
from jax.experimental import pallas as pl
from jax.experimental.pallas import tpu as pltpu
from jax.sharding import Mesh
from jax.sharding import PartitionSpec as P

TILE = 128
RANK = 128
CTILES = 32
DTILES = 64
NX = 4
NZ = 8
NCOL = 4
NDST = 32768
N_SLOTS = 256
SLOT_BITS, ROW_BITS, COL_BITS = 8, 5, 6
BLOCK = 64
UNROLL = 32
STEPS = 4
SORT_STEP = 16
SHIFTS = (0, 2, 1, 3)
GATHER_SHIFTS = (0, 1, 3, 2)
EPS = 1e-06

F32 = jnp.float32
BF16 = jnp.bfloat16
CORE, XPOS, COL = 0, 1, 2

SMEM = pl.BlockSpec(memory_space=pltpu.SMEM)
VMEM = pl.BlockSpec(memory_space=pltpu.VMEM)
HBM = pl.BlockSpec(memory_space=pltpu.HBM)
PARAMS = pltpu.CompilerParams(vmem_limit_bytes=40 * 2**20)


def tiles_of(n, dtype):
    return jax.ShapeDtypeStruct((n, TILE, RANK), dtype)


def each(n, body):
    whole = n // STEPS

    def step(i, carry):
        for j in range(STEPS):
            body(i * STEPS + j)
        return carry

    if whole > 1:
        lax.fori_loop(0, whole, step, 0)
    for i in range(whole * STEPS if whole > 1 else 0, n):
        body(i)


def accumulate(lo, hi, live, order, tiles, panel, acc, by_row, keep):
    dump = acc.shape[0] - 1

    def group(g, carry):
        for j in range(UNROLL):
            k = g * UNROLL + j
            code = order[N_SLOTS - 1 - k] if keep else order[k]
            row, col = (code >> SLOT_BITS) & (CTILES - 1), code >> (SLOT_BITS + ROW_BITS)
            dst, src = (row, col) if by_row else (col, row)
            tile, block = tiles[code & (N_SLOTS - 1)], panel[src]
            a, b = (tile, block) if by_row else (block, tile)
            acc[jnp.where(k < live, dst & (dump - 1), dump)] += jnp.dot(a, b, preferred_element_type=F32)
        return carry

    lax.fori_loop(lo, hi, group, 0)


def groups(n):
    return (n + UNROLL - 1) // UNROLL


def zero(acc):
    def one(i):
        acc[i] = jnp.zeros((TILE, RANK), F32)

    each(acc.shape[0], one)


def narrow(acc, out):
    def one(i):
        out[i] = acc[i].astype(BF16)

    each(out.shape[0], one)


def sort_slots(first, size, rows, cols, live, core, order, by_row, counts):
    bits = ROW_BITS if by_row else COL_BITS

    def several(g, carry):
        sends, keeps = carry
        slots = [first + g * SORT_STEP + j for j in range(SORT_STEP)]
        loaded = [(t, rows[t], cols[t]) for t in slots]
        for t, row, col in loaded:
            code = t + (row << SLOT_BITS) + (col << (SLOT_BITS + ROW_BITS))
            dst = row if by_row else col
            own = jnp.where(jnp.logical_and(t < live, dst >> (bits - 1) == core), 1, 0)
            order[jnp.where(own == 1, N_SLOTS - 1 - keeps, sends)] = code
            sends, keeps = sends + 1 - own, keeps + own
        return sends, keeps

    return lax.fori_loop(0, size // SORT_STEP, several, counts)


def sort_kernel(rows, cols, count, ids, after, order, numbers):
    live = count[0]
    counts = sort_slots(0, N_SLOTS, rows, cols, live, ids[CORE], order, False, (0, 0))
    numbers[0] = live - counts[1]
    numbers[1] = counts[1]


def sort_by_col(rows, cols, count, ids, after):
    words = lambda k: jax.ShapeDtypeStruct((k,), jnp.int32)
    return pl.pallas_call(
        sort_kernel,
        in_specs=[SMEM] * 4 + [pl.BlockSpec(memory_space=pl.ANY)],
        out_specs=[SMEM, SMEM],
        out_shape=[words(N_SLOTS), words(2)],
        cost_estimate=pl.CostEstimate(flops=2 * 10**9, bytes_accessed=4096, transcendentals=0),
        compiler_params=PARAMS,
        name="sort_by_col",
    )(rows, cols, count, ids, after)


def place(ids, parts, panel, axis, n, per):
    core, me = ids[CORE], ids[axis]
    for side in range(2):
        base = jnp.where(side == 0, core, 1 - core) * (n * per)
        for k in range(n):
            at = base + lax.rem(me + n - GATHER_SHIFTS[k], n) * per
            part = parts[side * n + k]

            def one(i):
                panel[at + i] = part[i]

            each(per, one)


def first_send_kernel(
    rows_hbm, cols_hbm, count, ids, tiles_hbm, panel_hbm, send, by_row, numbers, tiles, panel, rows, cols, acc, sems
):
    lists = [
        pltpu.make_async_copy(rows_hbm, rows, sems.at[0]),
        pltpu.make_async_copy(cols_hbm, cols, sems.at[1]),
    ]
    start = pltpu.make_async_copy(panel_hbm, panel, sems.at[2])
    blocks = [
        pltpu.make_async_copy(
            tiles_hbm.at[pl.ds(i * BLOCK, BLOCK)], tiles.at[pl.ds(i * BLOCK, BLOCK)], sems.at[3 + i]
        )
        for i in range(N_SLOTS // BLOCK)
    ]
    for copy in lists + [start] + blocks:
        copy.start()
    zero(acc)
    for copy in lists:
        copy.wait()
    live, core = count[0], ids[CORE]
    counts, done, last = (0, 0), 0, N_SLOTS // BLOCK - 1
    for i in range(last + 1):
        counts = sort_slots(i * BLOCK, BLOCK, rows, cols, live, core, by_row, True, counts)
        sends = jnp.minimum(live, (i + 1) * BLOCK) - counts[1]
        if i == 0:
            start.wait()
        blocks[i].wait()
        until = groups(sends) if i == last else sends // UNROLL
        accumulate(done, until, sends, by_row, tiles, panel, acc, True, False)
        done = until
    numbers[0] = live - counts[1]
    numbers[1] = counts[1]
    narrow(acc, send)


def in_hbm(value):
    return pltpu.with_memory_space_constraint(value, pltpu.HBM)


def first_send(rows, cols, count, ids, tiles, start):
    n = rows.shape[0]
    words = lambda k: jax.ShapeDtypeStruct((k,), jnp.int32)
    return pl.pallas_call(
        first_send_kernel,
        in_specs=[HBM, HBM, SMEM, SMEM, HBM, HBM],
        out_specs=[VMEM, SMEM, SMEM, VMEM, VMEM],
        out_shape=[tiles_of(CTILES // 2, BF16), words(n), words(2), tiles_of(n, BF16), tiles_of(DTILES, BF16)],
        scratch_shapes=[
            pltpu.SMEM((n,), jnp.int32),
            pltpu.SMEM((n,), jnp.int32),
            pltpu.VMEM((CTILES // 2 + 1, TILE, RANK), F32),
            pltpu.SemaphoreType.DMA((3 + n // BLOCK,)),
        ],
        compiler_params=PARAMS,
        name="first_send",
    )(*(in_hbm(v) for v in (rows, cols)), count, ids, *(in_hbm(v) for v in (tiles, start)))


def send_kernel(order, numbers, ids, tiles, *refs, by_row, axis, n, per):
    parts, (send, panel, acc) = refs[: 2 * n], refs[2 * n :]
    zero(acc)
    place(ids, parts, panel, axis, n, per)
    sends = numbers[0]
    accumulate(0, groups(sends), sends, order, tiles, panel, acc, by_row, False)
    narrow(acc, send)


def send_part(order, numbers, ids, tiles, parts, by_row, axis, name):
    n = len(parts) // 2
    per = parts[0].shape[0]
    half = (CTILES if by_row else DTILES) // 2
    return pl.pallas_call(
        functools.partial(send_kernel, by_row=by_row, axis=axis, n=n, per=per),
        in_specs=[SMEM] * 3 + [VMEM] * (1 + len(parts)),
        out_specs=[VMEM, VMEM],
        out_shape=[tiles_of(half, BF16), tiles_of(2 * n * per, BF16)],
        scratch_shapes=[pltpu.VMEM((half + 1, TILE, RANK), F32)],
        compiler_params=PARAMS,
        name=name,
    )(order, numbers, ids, tiles, *parts)


def keep_kernel(order, numbers, tiles, panel, keep, *squares, by_row):
    zero(keep)
    keeps = numbers[1]
    accumulate(0, groups(keeps), keeps, order, tiles, panel, keep, by_row, True)
    if squares:

        def one(i, total):
            block = panel[i].astype(F32)
            return total + jnp.sum((block * block).reshape(4, TILE // 4, RANK), axis=0)

        squares[0][...] = lax.fori_loop(0, DTILES, one, jnp.zeros((TILE // 4, RANK), F32))


def keep_part(order, numbers, tiles, panel, by_row, extra, name):
    half = (CTILES if by_row else DTILES) // 2
    work = 2 * N_SLOTS * TILE * TILE * RANK
    return pl.pallas_call(
        functools.partial(keep_kernel, by_row=by_row),
        in_specs=[SMEM, SMEM, VMEM, VMEM],
        out_specs=[VMEM] * (1 + len(extra)),
        out_shape=[tiles_of(half + 1, F32)] + extra,
        compiler_params=PARAMS,
        cost_estimate=pl.CostEstimate(flops=work, bytes_accessed=10 * 2**20, transcendentals=0),
        name=name,
    )(order, numbers, tiles, panel)


def pair_kernel(ids, keep, got, own, *sends, axis, n, per):
    me = ids[axis]
    for k in range(n):
        base = lax.rem(me + SHIFTS[k], n) * per

        def one(i):
            total = keep[base + i] + got[base + i].astype(F32)
            if k == 0:
                own[i] = total
            else:
                sends[k - 1][i] = total.astype(BF16)

        each(per, one)


def pair_sum(ids, keep, got, axis, n, per, name):
    return pl.pallas_call(
        functools.partial(pair_kernel, axis=axis, n=n, per=per),
        in_specs=[SMEM, VMEM, VMEM],
        out_specs=[VMEM] * n,
        out_shape=[tiles_of(per, F32)] + [tiles_of(per, BF16)] * (n - 1),
        compiler_params=PARAMS,
        name=name,
    )(ids, keep, got)


def caller_kernel(sorted_first, own, a, b, c, out):
    def one(i):
        total = own[i] + a[i].astype(F32) + b[i].astype(F32) + c[i].astype(F32)
        out[i] = total.astype(BF16).astype(F32).T.astype(BF16)

    each(own.shape[0], one)


def row_kernel(own, a, b, c, out):
    def one(i):
        total = own[i] + a[i].astype(F32) + b[i].astype(F32) + c[i].astype(F32)
        out[i] = total.astype(BF16)

    each(own.shape[0], one)


def four_sum(kernel, own, got, name):
    return pl.pallas_call(
        kernel,
        in_specs=[VMEM] * 4,
        out_specs=VMEM,
        out_shape=tiles_of(own.shape[0], BF16),
        compiler_params=PARAMS,
        name=name,
    )(own, *got)


def share_kernel(got, share, copies):
    total = got[0].astype(F32)
    for k in range(1, NZ):
        total += got[k].astype(F32)
    total = total.T
    share[...] = total
    for k in range(NZ):
        copies[k] = total.astype(BF16)


def last_pair_kernel(ids, keep, got, squares, own, *sends):
    me = ids[COL]
    per = CTILES // 2 // NCOL
    total = jnp.sum(squares[...], axis=0, keepdims=True)
    high = total.astype(BF16).astype(F32)
    middle = (total - high).astype(BF16).astype(F32)
    low = total - high - middle
    row = lax.broadcasted_iota(jnp.int32, (16, RANK), 0)
    coded = jnp.where(row == 0, high, jnp.where(row == 1, middle, jnp.where(row == 2, low, 0.0)))
    for k in range(NCOL):
        base = lax.rem(me + SHIFTS[k], NCOL) * per
        if k:
            sends[k - 1][pl.ds(per * TILE, 16), :] = coded.astype(BF16)
        for i in range(per):
            part = keep[base + i] + got[base + i].astype(F32)
            if k == 0:
                own[i] = part
            else:
                sends[k - 1][pl.ds(i * TILE, TILE), :] = part.astype(BF16)


def final_kernel(own, squares, share, a, b, c, caller, dest):
    per = CTILES // 2 // NCOL
    total = jnp.sum(squares[...], axis=0, keepdims=True)
    for got in (a, b, c):
        total += jnp.sum(got[pl.ds(per * TILE, 16), :].astype(F32), axis=0, keepdims=True)
    scale = lax.rsqrt(total / NDST + EPS)
    dest[...] = (share[...] * scale).astype(BF16)
    for i in range(per):
        at = pl.ds(i * TILE, TILE)
        part = own[i] + a[at, :].astype(F32) + b[at, :].astype(F32) + c[at, :].astype(F32)
        caller[at, :] = (part * scale).astype(BF16)


def shifted(value, axis, k, n):
    return lax.ppermute(value, axis, [(i, (i + k) % n) for i in range(n)])


def swap(value):
    return lax.ppermute(value, "layer", [(0, 1), (1, 0)])


def exchange(values, axis, n):
    return [shifted(v, axis, k, n) for v, k in zip(values, SHIFTS[1:], strict=True)]


def gather(value, axis, n):
    mine = [value] + [shifted(value, axis, k, n) for k in GATHER_SHIFTS[1:]]
    return mine + [swap(v) for v in mine]


def on_device(tile_values, tile_rows, tile_cols, tile_count, start_panel):
    tiles = tile_values[0, 0, 0]
    rows = tile_rows[0, 0, 0]
    cols = tile_cols[0, 0, 0]
    count = tile_count[0, 0]
    ids = jnp.stack([lax.axis_index(a) for a in ("layer", "x", "col")]).astype(jnp.int32)
    start = start_panel.reshape(DTILES, TILE, RANK)
    quarter = CTILES // 2 // NCOL

    send, by_row, row_numbers, tiles, panel = first_send(rows, cols, count, ids, tiles, start)
    got = swap(send)
    [keep] = keep_part(by_row, row_numbers, tiles, panel, True, [], "first_keep")
    own, *sends = pair_sum(ids, keep, got, COL, NCOL, quarter, "first_pair")
    by_col, col_numbers = sort_by_col(rows, cols, count, ids, own)
    part = pl.pallas_call(
        caller_kernel,
        in_specs=[SMEM] + [VMEM] * NCOL,
        out_specs=VMEM,
        out_shape=tiles_of(quarter, BF16),
        compiler_params=PARAMS,
        name="first_sum",
    )(col_numbers, own, *exchange(sends, "col", NCOL))
    parts = gather(part, "col", NCOL)

    send, panel = send_part(by_col, col_numbers, ids, tiles, parts, False, COL, "back_send")
    got = swap(send)
    [keep] = keep_part(by_col, col_numbers, tiles, panel, False, [], "back_keep")
    own, *sends = pair_sum(ids, keep, got, XPOS, NX, NZ, "back_pair")
    part = four_sum(row_kernel, own, exchange(sends, "x", NX), "back_sum")
    got = lax.all_to_all(part, "z", split_axis=0, concat_axis=0, tiled=True)
    share, copies = pl.pallas_call(
        share_kernel,
        in_specs=[VMEM],
        out_specs=[VMEM, VMEM],
        out_shape=[jax.ShapeDtypeStruct((TILE, RANK), F32), tiles_of(NZ, BF16)],
        compiler_params=PARAMS,
        name="share_sum",
    )(got)
    part = lax.all_to_all(copies, "z", split_axis=0, concat_axis=0, tiled=True)
    parts = gather(part, "x", NX)

    send, panel = send_part(by_row, row_numbers, ids, tiles, parts, True, XPOS, "last_send")
    got = swap(send)
    keep, squares = keep_part(
        by_row, row_numbers, tiles, panel, True, [jax.ShapeDtypeStruct((TILE // 4, RANK), F32)], "last_keep"
    )
    chunk = jax.ShapeDtypeStruct((quarter * TILE + 16, RANK), BF16)
    own, *sends = pl.pallas_call(
        last_pair_kernel,
        in_specs=[SMEM, VMEM, VMEM, VMEM],
        out_specs=[VMEM] * NCOL,
        out_shape=[tiles_of(quarter, F32)] + [chunk] * (NCOL - 1),
        compiler_params=PARAMS,
        name="last_pair",
    )(ids, keep, got, squares)
    got = exchange(sends, "col", NCOL)
    caller, dest = pl.pallas_call(
        final_kernel,
        in_specs=[VMEM] * 6,
        out_specs=[VMEM, VMEM],
        out_shape=[
            jax.ShapeDtypeStruct((quarter * TILE, RANK), BF16),
            jax.ShapeDtypeStruct((TILE, RANK), BF16),
        ],
        compiler_params=PARAMS,
        name="final",
    )(own, squares, share, *got)
    return caller[None], dest[None]


def solution(mesh):
    fine = Mesh(mesh.devices.reshape(2, NX, NZ, NCOL), ("layer", "x", "z", "col"))
    row = ("x", "z")
    placed = (
        P("layer", row, "col", None, None, None),
        P("layer", row, "col", None),
        P("layer", row, "col", None),
        P("layer", row, "col"),
        P("col", None),
    )
    return jax.shard_map(
        on_device,
        mesh=fine,
        in_specs=placed,
        out_specs=(P(row, ("layer", "col"), None), P("col", ("layer", "x", "z"), None)),
        check_vma=False,
    )
```

```python
import functools

import jax
import jax.numpy as jnp
from jax import lax
from jax.experimental import pallas as pl
from jax.experimental.pallas import tpu as pltpu
from jax.sharding import Mesh
from jax.sharding import PartitionSpec as P

TILE = 128
RANK = 128
CTILES = 32
DTILES = 64
NX = 4
NZ = 8
NCOL = 4
NDST = 32768
N_SLOTS = 256
SLOT_BITS, ROW_BITS, COL_BITS = 8, 5, 6
BLOCK = 64
UNROLL = 32
STEPS = 4
SORT_STEP = 16
SHIFTS = (0, 2, 1, 3)
GATHER_SHIFTS = (0, 1, 3, 2)
EPS = 1e-06

F32 = jnp.float32
BF16 = jnp.bfloat16
CORE, XPOS, COL = 0, 1, 2

SMEM = pl.BlockSpec(memory_space=pltpu.SMEM)
VMEM = pl.BlockSpec(memory_space=pltpu.VMEM)
HBM = pl.BlockSpec(memory_space=pltpu.HBM)
PARAMS = pltpu.CompilerParams(vmem_limit_bytes=40 * 2**20)


def tiles_of(n, dtype):
    return jax.ShapeDtypeStruct((n, TILE, RANK), dtype)


def each(n, body):
    whole = n // STEPS

    def step(i, carry):
        for j in range(STEPS):
            body(i * STEPS + j)
        return carry

    if whole > 1:
        lax.fori_loop(0, whole, step, 0)
    for i in range(whole * STEPS if whole > 1 else 0, n):
        body(i)


def accumulate(lo, hi, live, order, tiles, panel, acc, by_row, keep):
    dump = acc.shape[0] - 1

    def group(g, carry):
        for j in range(UNROLL):
            k = g * UNROLL + j
            code = order[N_SLOTS - 1 - k] if keep else order[k]
            row, col = (code >> SLOT_BITS) & (CTILES - 1), code >> (SLOT_BITS + ROW_BITS)
            dst, src = (row, col) if by_row else (col, row)
            tile, block = tiles[code & (N_SLOTS - 1)], panel[src]
            a, b = (tile, block) if by_row else (block, tile)
            acc[jnp.where(k < live, dst & (dump - 1), dump)] += jnp.dot(a, b, preferred_element_type=F32)
        return carry

    lax.fori_loop(lo, hi, group, 0)


def groups(n):
    return (n + UNROLL - 1) // UNROLL


def zero(acc):
    def one(i):
        acc[i] = jnp.zeros((TILE, RANK), F32)

    each(acc.shape[0], one)


def narrow(acc, out):
    def one(i):
        out[i] = acc[i].astype(BF16)

    each(out.shape[0], one)


def sort_slots(first, size, rows, cols, live, core, order, by_row, counts):
    bits = ROW_BITS if by_row else COL_BITS

    def several(g, carry):
        sends, keeps = carry
        slots = [first + g * SORT_STEP + j for j in range(SORT_STEP)]
        loaded = [(t, rows[t], cols[t]) for t in slots]
        for t, row, col in loaded:
            code = t + (row << SLOT_BITS) + (col << (SLOT_BITS + ROW_BITS))
            dst = row if by_row else col
            own = jnp.where(jnp.logical_and(t < live, dst >> (bits - 1) == core), 1, 0)
            order[jnp.where(own == 1, N_SLOTS - 1 - keeps, sends)] = code
            sends, keeps = sends + 1 - own, keeps + own
        return sends, keeps

    return lax.fori_loop(0, size // SORT_STEP, several, counts)


def sort_kernel(rows, cols, count, ids, after, order, numbers, *, by_row):
    live = count[0]
    counts = sort_slots(0, N_SLOTS, rows, cols, live, ids[CORE], order, by_row, (0, 0))
    numbers[0] = live - counts[1]
    numbers[1] = counts[1]


def sort_list(rows, cols, count, ids, after, by_row, name):
    words = lambda k: jax.ShapeDtypeStruct((k,), jnp.int32)
    return pl.pallas_call(
        functools.partial(sort_kernel, by_row=by_row),
        in_specs=[SMEM] * 4 + [pl.BlockSpec(memory_space=pl.ANY)],
        out_specs=[SMEM, SMEM],
        out_shape=[words(N_SLOTS), words(2)],
        cost_estimate=pl.CostEstimate(flops=2 * 10**9, bytes_accessed=4096, transcendentals=0),
        compiler_params=PARAMS,
        name=name,
    )(rows, cols, count, ids, after)


def place(ids, parts, panel, axis, n, per):
    core, me = ids[CORE], ids[axis]
    for side in range(2):
        base = jnp.where(side == 0, core, 1 - core) * (n * per)
        for k in range(n):
            at = base + lax.rem(me + n - GATHER_SHIFTS[k], n) * per
            part = parts[side * n + k]

            def one(i):
                panel[at + i] = part[i]

            each(per, one)


def accumulate_slots(first, size, dst, src, count, tiles, panel, acc):
    live = count[0]
    left = jnp.clip(live - first, 0, size)

    def group(g, carry):
        for j in range(UNROLL):
            t = first + g * UNROLL + j
            d = jnp.where(t < live, dst[t], CTILES)
            acc[d] += jnp.dot(tiles[t], panel[src[t]], preferred_element_type=F32)
        return carry

    lax.fori_loop(0, (left + UNROLL - 1) // UNROLL, group, 0)


def split(ids, acc, keep, send, half):
    core = ids[CORE]

    def one(i):
        keep[i] = acc[core * half + i]
        send[i] = acc[(1 - core) * half + i].astype(BF16)

    each(half, one)


def first_kernel(dst_hbm, src_hbm, count, ids, tiles_hbm, panel_hbm, keep, send, tiles, dst, src, panel, acc, sems):
    n_blocks = tiles.shape[0] // BLOCK
    lists = [
        pltpu.make_async_copy(dst_hbm, dst, sems.at[0]),
        pltpu.make_async_copy(src_hbm, src, sems.at[1]),
        pltpu.make_async_copy(panel_hbm, panel, sems.at[2]),
    ]
    blocks = [
        pltpu.make_async_copy(
            tiles_hbm.at[pl.ds(i * BLOCK, BLOCK)], tiles.at[pl.ds(i * BLOCK, BLOCK)], sems.at[3 + i]
        )
        for i in range(n_blocks)
    ]
    for copy in lists + blocks:
        copy.start()
    zero(acc)
    for copy in lists:
        copy.wait()
    for i in range(n_blocks):
        blocks[i].wait()
        accumulate_slots(i * BLOCK, BLOCK, dst, src, count, tiles, panel, acc)
    split(ids, acc, keep, send, CTILES // 2)


def in_hbm(value):
    return pltpu.with_memory_space_constraint(value, pltpu.HBM)


def first_pass(rows, cols, count, ids, tiles, start):
    return pl.pallas_call(
        first_kernel,
        in_specs=[HBM, HBM, SMEM, SMEM, HBM, HBM],
        out_specs=[VMEM] * 3,
        out_shape=[tiles_of(CTILES // 2, F32), tiles_of(CTILES // 2, BF16), tiles_of(tiles.shape[0], BF16)],
        scratch_shapes=[
            pltpu.SMEM(rows.shape, jnp.int32),
            pltpu.SMEM(cols.shape, jnp.int32),
            pltpu.VMEM(start.shape, BF16),
            pltpu.VMEM((CTILES + 1, TILE, RANK), F32),
            pltpu.SemaphoreType.DMA((3 + tiles.shape[0] // BLOCK,)),
        ],
        compiler_params=pltpu.CompilerParams(vmem_limit_bytes=40 * 2**20),
        name="first_pass",
    )(*(in_hbm(v) for v in (rows, cols)), count, ids, *(in_hbm(v) for v in (tiles, start)))


def send_kernel(order, numbers, ids, tiles, *refs, by_row, axis, n, per):
    parts, (send, panel, acc) = refs[: 2 * n], refs[2 * n :]
    zero(acc)
    place(ids, parts, panel, axis, n, per)
    sends = numbers[0]
    accumulate(0, groups(sends), sends, order, tiles, panel, acc, by_row, False)
    narrow(acc, send)


def send_part(order, numbers, ids, tiles, parts, by_row, axis, name):
    n = len(parts) // 2
    per = parts[0].shape[0]
    half = (CTILES if by_row else DTILES) // 2
    return pl.pallas_call(
        functools.partial(send_kernel, by_row=by_row, axis=axis, n=n, per=per),
        in_specs=[SMEM] * 3 + [VMEM] * (1 + len(parts)),
        out_specs=[VMEM, VMEM],
        out_shape=[tiles_of(half, BF16), tiles_of(2 * n * per, BF16)],
        scratch_shapes=[pltpu.VMEM((half + 1, TILE, RANK), F32)],
        compiler_params=PARAMS,
        name=name,
    )(order, numbers, ids, tiles, *parts)


def keep_kernel(order, numbers, tiles, panel, keep, *squares, by_row):
    zero(keep)
    keeps = numbers[1]
    accumulate(0, groups(keeps), keeps, order, tiles, panel, keep, by_row, True)
    if squares:

        def one(i, total):
            block = panel[i].astype(F32)
            return total + jnp.sum((block * block).reshape(4, TILE // 4, RANK), axis=0)

        squares[0][...] = lax.fori_loop(0, DTILES, one, jnp.zeros((TILE // 4, RANK), F32))


def keep_part(order, numbers, tiles, panel, by_row, extra, name):
    half = (CTILES if by_row else DTILES) // 2
    work = 2 * N_SLOTS * TILE * TILE * RANK
    return pl.pallas_call(
        functools.partial(keep_kernel, by_row=by_row),
        in_specs=[SMEM, SMEM, VMEM, VMEM],
        out_specs=[VMEM] * (1 + len(extra)),
        out_shape=[tiles_of(half + 1, F32)] + extra,
        compiler_params=PARAMS,
        cost_estimate=pl.CostEstimate(flops=work, bytes_accessed=10 * 2**20, transcendentals=0),
        name=name,
    )(order, numbers, tiles, panel)


def pair_kernel(ids, keep, got, own, *sends, axis, n, per):
    me = ids[axis]
    for k in range(n):
        base = lax.rem(me + SHIFTS[k], n) * per

        def one(i):
            total = keep[base + i] + got[base + i].astype(F32)
            if k == 0:
                own[i] = total
            else:
                sends[k - 1][i] = total.astype(BF16)

        each(per, one)


def pair_sum(ids, keep, got, axis, n, per, name):
    return pl.pallas_call(
        functools.partial(pair_kernel, axis=axis, n=n, per=per),
        in_specs=[SMEM, VMEM, VMEM],
        out_specs=[VMEM] * n,
        out_shape=[tiles_of(per, F32)] + [tiles_of(per, BF16)] * (n - 1),
        compiler_params=PARAMS,
        name=name,
    )(ids, keep, got)


def caller_kernel(sorted_first, own, a, b, c, out):
    def one(i):
        total = own[i] + a[i].astype(F32) + b[i].astype(F32) + c[i].astype(F32)
        out[i] = total.astype(BF16).astype(F32).T.astype(BF16)

    each(own.shape[0], one)


def row_kernel(sorted_first, own, a, b, c, out):
    def one(i):
        total = own[i] + a[i].astype(F32) + b[i].astype(F32) + c[i].astype(F32)
        out[i] = total.astype(BF16)

    each(own.shape[0], one)


def four_sum(kernel, sorted_first, own, got, name):
    return pl.pallas_call(
        kernel,
        in_specs=[SMEM] + [VMEM] * 4,
        out_specs=VMEM,
        out_shape=tiles_of(own.shape[0], BF16),
        compiler_params=PARAMS,
        name=name,
    )(sorted_first, own, *got)


def share_kernel(got, share, copies):
    total = got[0].astype(F32)
    for k in range(1, NZ):
        total += got[k].astype(F32)
    total = total.T
    share[...] = total
    for k in range(NZ):
        copies[k] = total.astype(BF16)


def last_pair_kernel(ids, keep, got, squares, own, *sends):
    me = ids[COL]
    per = CTILES // 2 // NCOL
    total = jnp.sum(squares[...], axis=0, keepdims=True)
    high = total.astype(BF16).astype(F32)
    middle = (total - high).astype(BF16).astype(F32)
    low = total - high - middle
    row = lax.broadcasted_iota(jnp.int32, (16, RANK), 0)
    coded = jnp.where(row == 0, high, jnp.where(row == 1, middle, jnp.where(row == 2, low, 0.0)))
    for k in range(NCOL):
        base = lax.rem(me + SHIFTS[k], NCOL) * per
        if k:
            sends[k - 1][pl.ds(per * TILE, 16), :] = coded.astype(BF16)
        for i in range(per):
            part = keep[base + i] + got[base + i].astype(F32)
            if k == 0:
                own[i] = part
            else:
                sends[k - 1][pl.ds(i * TILE, TILE), :] = part.astype(BF16)


def final_kernel(own, squares, share, a, b, c, caller, dest):
    per = CTILES // 2 // NCOL
    total = jnp.sum(squares[...], axis=0, keepdims=True)
    for got in (a, b, c):
        total += jnp.sum(got[pl.ds(per * TILE, 16), :].astype(F32), axis=0, keepdims=True)
    scale = lax.rsqrt(total / NDST + EPS)
    dest[...] = (share[...] * scale).astype(BF16)
    for i in range(per):
        at = pl.ds(i * TILE, TILE)
        part = own[i] + a[at, :].astype(F32) + b[at, :].astype(F32) + c[at, :].astype(F32)
        caller[at, :] = (part * scale).astype(BF16)


def shifted(value, axis, k, n):
    return lax.ppermute(value, axis, [(i, (i + k) % n) for i in range(n)])


def swap(value):
    return lax.ppermute(value, "layer", [(0, 1), (1, 0)])


def exchange(values, axis, n):
    return [shifted(v, axis, k, n) for v, k in zip(values, SHIFTS[1:], strict=True)]


def gather(value, axis, n):
    mine = [value] + [shifted(value, axis, k, n) for k in GATHER_SHIFTS[1:]]
    return mine + [swap(v) for v in mine]


def on_device(tile_values, tile_rows, tile_cols, tile_count, start_panel):
    tiles = tile_values[0, 0, 0]
    rows = tile_rows[0, 0, 0]
    cols = tile_cols[0, 0, 0]
    count = tile_count[0, 0]
    ids = jnp.stack([lax.axis_index(a) for a in ("layer", "x", "col")]).astype(jnp.int32)
    start = start_panel.reshape(DTILES, TILE, RANK)
    quarter = CTILES // 2 // NCOL

    keep, send, tiles = first_pass(rows, cols, count, ids, tiles, start)
    own, *sends = pair_sum(ids, keep, swap(send), COL, NCOL, quarter, "first_pair")
    by_col, col_numbers = sort_list(rows, cols, count, ids, own, False, "sort_by_col")
    part = four_sum(caller_kernel, col_numbers, own, exchange(sends, "col", NCOL), "first_sum")
    parts = gather(part, "col", NCOL)

    send, panel = send_part(by_col, col_numbers, ids, tiles, parts, False, COL, "back_send")
    got = swap(send)
    [keep] = keep_part(by_col, col_numbers, tiles, panel, False, [], "back_keep")
    own, *sends = pair_sum(ids, keep, got, XPOS, NX, NZ, "back_pair")
    by_row, row_numbers = sort_list(rows, cols, count, ids, own, True, "sort_by_row")
    part = four_sum(row_kernel, row_numbers, own, exchange(sends, "x", NX), "back_sum")
    got = lax.all_to_all(part, "z", split_axis=0, concat_axis=0, tiled=True)
    share, copies = pl.pallas_call(
        share_kernel,
        in_specs=[VMEM],
        out_specs=[VMEM, VMEM],
        out_shape=[jax.ShapeDtypeStruct((TILE, RANK), F32), tiles_of(NZ, BF16)],
        compiler_params=PARAMS,
        name="share_sum",
    )(got)
    part = lax.all_to_all(copies, "z", split_axis=0, concat_axis=0, tiled=True)
    parts = gather(part, "x", NX)

    send, panel = send_part(by_row, row_numbers, ids, tiles, parts, True, XPOS, "last_send")
    got = swap(send)
    keep, squares = keep_part(
        by_row, row_numbers, tiles, panel, True, [jax.ShapeDtypeStruct((TILE // 4, RANK), F32)], "last_keep"
    )
    chunk = jax.ShapeDtypeStruct((quarter * TILE + 16, RANK), BF16)
    own, *sends = pl.pallas_call(
        last_pair_kernel,
        in_specs=[SMEM, VMEM, VMEM, VMEM],
        out_specs=[VMEM] * NCOL,
        out_shape=[tiles_of(quarter, F32)] + [chunk] * (NCOL - 1),
        compiler_params=PARAMS,
        name="last_pair",
    )(ids, keep, got, squares)
    got = exchange(sends, "col", NCOL)
    caller, dest = pl.pallas_call(
        final_kernel,
        in_specs=[VMEM] * 6,
        out_specs=[VMEM, VMEM],
        out_shape=[
            jax.ShapeDtypeStruct((quarter * TILE, RANK), BF16),
            jax.ShapeDtypeStruct((TILE, RANK), BF16),
        ],
        compiler_params=PARAMS,
        name="final",
    )(own, squares, share, *got)
    return caller[None], dest[None]


def solution(mesh):
    fine = Mesh(mesh.devices.reshape(2, NX, NZ, NCOL), ("layer", "x", "z", "col"))
    row = ("x", "z")
    placed = (
        P("layer", row, "col", None, None, None),
        P("layer", row, "col", None),
        P("layer", row, "col", None),
        P("layer", row, "col"),
        P("col", None),
    )
    return jax.shard_map(
        on_device,
        mesh=fine,
        in_specs=placed,
        out_specs=(P(row, ("layer", "col"), None), P("col", ("layer", "x", "z"), None)),
        check_vma=False,
    )
```

```python
import functools

import jax
import jax.numpy as jnp
from jax import lax
from jax.experimental import pallas as pl
from jax.experimental.pallas import tpu as pltpu
from jax.sharding import Mesh
from jax.sharding import PartitionSpec as P

TILE = 128
RANK = 128
CTILES = 32
DTILES = 64
NX = 4
NZ = 8
NCOL = 4
NDST = 32768
N_SLOTS = 256
SLOT_BITS, ROW_BITS, COL_BITS = 8, 5, 6
BLOCK = 32
UNROLL = 32
STEPS = 4
SORT_STEP = 16
SHIFTS = (0, 2, 1, 3)
GATHER_SHIFTS = (0, 1, 3, 2)
EPS = 1e-06

F32 = jnp.float32
BF16 = jnp.bfloat16
CORE, XPOS, COL = 0, 1, 2

SMEM = pl.BlockSpec(memory_space=pltpu.SMEM)
VMEM = pl.BlockSpec(memory_space=pltpu.VMEM)
HBM = pl.BlockSpec(memory_space=pltpu.HBM)
ANY = pl.BlockSpec(memory_space=pl.ANY)
PARAMS = pltpu.CompilerParams(vmem_limit_bytes=40 * 2**20)


def tiles_of(n, dtype):
    return jax.ShapeDtypeStruct((n, TILE, RANK), dtype)


def each(n, body):
    whole = n // STEPS

    def step(i, carry):
        for j in range(STEPS):
            body(i * STEPS + j)
        return carry

    if whole > 1:
        lax.fori_loop(0, whole, step, 0)
    for i in range(whole * STEPS if whole > 1 else 0, n):
        body(i)


def accumulate(lo, hi, live, order, tiles, panel, acc, by_row, keep):
    dump = acc.shape[0] - 1

    def group(g, carry):
        for j in range(UNROLL):
            k = g * UNROLL + j
            code = order[N_SLOTS - 1 - k] if keep else order[k]
            row, col = (code >> SLOT_BITS) & (CTILES - 1), code >> (SLOT_BITS + ROW_BITS)
            dst, src = (row, col) if by_row else (col, row)
            tile, block = tiles[code & (N_SLOTS - 1)], panel[src]
            a, b = (tile, block) if by_row else (block, tile)
            acc[jnp.where(k < live, dst & (dump - 1), dump)] += jnp.dot(a, b, preferred_element_type=F32)
        return carry

    lax.fori_loop(lo, hi, group, 0)


def groups(n):
    return (n + UNROLL - 1) // UNROLL


def zero(acc):
    def one(i):
        acc[i] = jnp.zeros((TILE, RANK), F32)

    each(acc.shape[0], one)


def narrow(acc, out):
    def one(i):
        out[i] = acc[i].astype(BF16)

    each(out.shape[0], one)


def sort_slots(first, size, rows, cols, live, core, order, by_row, counts):
    bits = ROW_BITS if by_row else COL_BITS

    def several(g, carry):
        sends, keeps = carry
        slots = [first + g * SORT_STEP + j for j in range(SORT_STEP)]
        loaded = [(t, rows[t], cols[t]) for t in slots]
        for t, row, col in loaded:
            code = t + (row << SLOT_BITS) + (col << (SLOT_BITS + ROW_BITS))
            dst = row if by_row else col
            own = jnp.where(jnp.logical_and(t < live, dst >> (bits - 1) == core), 1, 0)
            order[jnp.where(own == 1, N_SLOTS - 1 - keeps, sends)] = code
            sends, keeps = sends + 1 - own, keeps + own
        return sends, keeps

    return lax.fori_loop(0, size // SORT_STEP, several, counts)


def sort_kernel(rows, cols, count, ids, after, order, numbers, *, by_row):
    live = count[0]
    counts = sort_slots(0, N_SLOTS, rows, cols, live, ids[CORE], order, by_row, (0, 0))
    numbers[0] = live - counts[1]
    numbers[1] = counts[1]


def sort_list(rows, cols, count, ids, after, by_row, name):
    words = lambda k: jax.ShapeDtypeStruct((k,), jnp.int32)
    return pl.pallas_call(
        functools.partial(sort_kernel, by_row=by_row),
        in_specs=[SMEM] * 4 + [ANY],
        out_specs=[SMEM, SMEM],
        out_shape=[words(N_SLOTS), words(2)],
        cost_estimate=pl.CostEstimate(flops=2 * 10**9, bytes_accessed=4096, transcendentals=0),
        compiler_params=PARAMS,
        name=name,
    )(rows, cols, count, ids, after)


def place(ids, parts, panel, axis, n, per):
    core, me = ids[CORE], ids[axis]
    for side in range(2):
        base = jnp.where(side == 0, core, 1 - core) * (n * per)
        for k in range(n):
            at = base + lax.rem(me + n - GATHER_SHIFTS[k], n) * per
            part = parts[side * n + k]

            def one(i):
                panel[at + i] = part[i]

            each(per, one)


def accumulate_slots(first, size, dst, src, count, tiles, panel, acc):
    live = count[0]
    left = jnp.clip(live - first, 0, size)

    def group(g, carry):
        for j in range(UNROLL):
            t = first + g * UNROLL + j
            d = jnp.where(t < live, dst[t], CTILES)
            acc[d] += jnp.dot(tiles[t], panel[src[t]], preferred_element_type=F32)
        return carry

    lax.fori_loop(0, (left + UNROLL - 1) // UNROLL, group, 0)


def split(ids, acc, keep, send, half):
    core = ids[CORE]

    def one(i):
        keep[i] = acc[core * half + i]
        send[i] = acc[(1 - core) * half + i].astype(BF16)

    each(half, one)


def first_kernel(dst_hbm, src_hbm, count, ids, tiles_hbm, panel_hbm, keep, send, tiles, dst, src, panel, acc, sems):
    n_blocks = tiles.shape[0] // BLOCK
    lists = [
        pltpu.make_async_copy(dst_hbm, dst, sems.at[0]),
        pltpu.make_async_copy(src_hbm, src, sems.at[1]),
        pltpu.make_async_copy(panel_hbm, panel, sems.at[2]),
    ]
    blocks = [
        pltpu.make_async_copy(
            tiles_hbm.at[pl.ds(i * BLOCK, BLOCK)], tiles.at[pl.ds(i * BLOCK, BLOCK)], sems.at[3 + i]
        )
        for i in range(n_blocks)
    ]
    for copy in lists + blocks:
        copy.start()
    zero(acc)
    for copy in lists:
        copy.wait()
    for i in range(n_blocks):
        blocks[i].wait()
        accumulate_slots(i * BLOCK, BLOCK, dst, src, count, tiles, panel, acc)
    split(ids, acc, keep, send, CTILES // 2)


def in_hbm(value):
    return pltpu.with_memory_space_constraint(value, pltpu.HBM)


def first_pass(rows, cols, count, ids, tiles, start):
    return pl.pallas_call(
        first_kernel,
        in_specs=[HBM, HBM, SMEM, SMEM, HBM, HBM],
        out_specs=[VMEM] * 3,
        out_shape=[tiles_of(CTILES // 2, F32), tiles_of(CTILES // 2, BF16), tiles_of(tiles.shape[0], BF16)],
        scratch_shapes=[
            pltpu.SMEM(rows.shape, jnp.int32),
            pltpu.SMEM(cols.shape, jnp.int32),
            pltpu.VMEM(start.shape, BF16),
            pltpu.VMEM((CTILES + 1, TILE, RANK), F32),
            pltpu.SemaphoreType.DMA((3 + tiles.shape[0] // BLOCK,)),
        ],
        compiler_params=pltpu.CompilerParams(vmem_limit_bytes=40 * 2**20),
        name="first_pass",
    )(*(in_hbm(v) for v in (rows, cols)), count, ids, *(in_hbm(v) for v in (tiles, start)))


def send_kernel(order, numbers, ids, tiles, *refs, by_row, axis, n, per):
    parts, (send, panel, acc) = refs[: 2 * n], refs[2 * n :]
    zero(acc)
    place(ids, parts, panel, axis, n, per)
    sends = numbers[0]
    accumulate(0, groups(sends), sends, order, tiles, panel, acc, by_row, False)
    narrow(acc, send)


def send_part(order, numbers, ids, tiles, parts, by_row, axis, name):
    n = len(parts) // 2
    per = parts[0].shape[0]
    half = (CTILES if by_row else DTILES) // 2
    return pl.pallas_call(
        functools.partial(send_kernel, by_row=by_row, axis=axis, n=n, per=per),
        in_specs=[SMEM] * 3 + [VMEM] * (1 + len(parts)),
        out_specs=[VMEM, VMEM],
        out_shape=[tiles_of(half, BF16), tiles_of(2 * n * per, BF16)],
        scratch_shapes=[pltpu.VMEM((half + 1, TILE, RANK), F32)],
        compiler_params=PARAMS,
        name=name,
    )(order, numbers, ids, tiles, *parts)


def keep_kernel(order, numbers, tiles, panel, keep, *squares, by_row):
    zero(keep)
    keeps = numbers[1]
    accumulate(0, groups(keeps), keeps, order, tiles, panel, keep, by_row, True)
    if squares:

        def one(i, total):
            block = panel[i].astype(F32)
            return total + jnp.sum((block * block).reshape(4, TILE // 4, RANK), axis=0)

        squares[0][...] = lax.fori_loop(0, DTILES, one, jnp.zeros((TILE // 4, RANK), F32))


def keep_part(order, numbers, tiles, panel, by_row, extra, name):
    half = (CTILES if by_row else DTILES) // 2
    work = 2 * N_SLOTS * TILE * TILE * RANK
    return pl.pallas_call(
        functools.partial(keep_kernel, by_row=by_row),
        in_specs=[SMEM, SMEM, VMEM, VMEM],
        out_specs=[VMEM] * (1 + len(extra)),
        out_shape=[tiles_of(half + 1, F32)] + extra,
        compiler_params=PARAMS,
        cost_estimate=pl.CostEstimate(flops=work, bytes_accessed=10 * 2**20, transcendentals=0),
        name=name,
    )(order, numbers, tiles, panel)


def pair_kernel(ids, keep, got, own, *sends, axis, n, per):
    me = ids[axis]
    for k in range(n):
        base = lax.rem(me + SHIFTS[k], n) * per

        def one(i):
            total = keep[base + i] + got[base + i].astype(F32)
            if k == 0:
                own[i] = total
            else:
                sends[k - 1][i] = total.astype(BF16)

        each(per, one)


def pair_sum(ids, keep, got, axis, n, per, name):
    return pl.pallas_call(
        functools.partial(pair_kernel, axis=axis, n=n, per=per),
        in_specs=[SMEM, VMEM, VMEM],
        out_specs=[VMEM] * n,
        out_shape=[tiles_of(per, F32)] + [tiles_of(per, BF16)] * (n - 1),
        compiler_params=PARAMS,
        name=name,
    )(ids, keep, got)


def caller_kernel(sorted_first, own, a, b, c, out):
    def one(i):
        total = own[i] + a[i].astype(F32) + b[i].astype(F32) + c[i].astype(F32)
        out[i] = total.astype(BF16).astype(F32).T.astype(BF16)

    each(own.shape[0], one)


def row_kernel(sorted_first, own, a, b, c, out):
    def one(i):
        total = own[i] + a[i].astype(F32) + b[i].astype(F32) + c[i].astype(F32)
        out[i] = total.astype(BF16)

    each(own.shape[0], one)


def four_sum(kernel, sorted_first, own, got, name):
    return pl.pallas_call(
        kernel,
        in_specs=[ANY] + [VMEM] * 4,
        out_specs=VMEM,
        out_shape=tiles_of(own.shape[0], BF16),
        compiler_params=PARAMS,
        name=name,
    )(sorted_first, own, *got)


def share_kernel(got, share, copies):
    total = got[0].astype(F32)
    for k in range(1, NZ):
        total += got[k].astype(F32)
    total = total.T
    share[...] = total
    for k in range(NZ):
        copies[k] = total.astype(BF16)


def last_pair_kernel(ids, keep, got, squares, own, *sends):
    me = ids[COL]
    per = CTILES // 2 // NCOL
    total = jnp.sum(squares[...], axis=0, keepdims=True)
    high = total.astype(BF16).astype(F32)
    middle = (total - high).astype(BF16).astype(F32)
    low = total - high - middle
    row = lax.broadcasted_iota(jnp.int32, (16, RANK), 0)
    coded = jnp.where(row == 0, high, jnp.where(row == 1, middle, jnp.where(row == 2, low, 0.0)))
    for k in range(NCOL):
        base = lax.rem(me + SHIFTS[k], NCOL) * per
        if k:
            sends[k - 1][pl.ds(per * TILE, 16), :] = coded.astype(BF16)
        for i in range(per):
            part = keep[base + i] + got[base + i].astype(F32)
            if k == 0:
                own[i] = part
            else:
                sends[k - 1][pl.ds(i * TILE, TILE), :] = part.astype(BF16)


def final_kernel(own, squares, share, a, b, c, caller, dest):
    per = CTILES // 2 // NCOL
    total = jnp.sum(squares[...], axis=0, keepdims=True)
    for got in (a, b, c):
        total += jnp.sum(got[pl.ds(per * TILE, 16), :].astype(F32), axis=0, keepdims=True)
    scale = lax.rsqrt(total / NDST + EPS)
    dest[...] = (share[...] * scale).astype(BF16)
    for i in range(per):
        at = pl.ds(i * TILE, TILE)
        part = own[i] + a[at, :].astype(F32) + b[at, :].astype(F32) + c[at, :].astype(F32)
        caller[at, :] = (part * scale).astype(BF16)


def shifted(value, axis, k, n):
    return lax.ppermute(value, axis, [(i, (i + k) % n) for i in range(n)])


def swap(value):
    return lax.ppermute(value, "layer", [(0, 1), (1, 0)])


def exchange(values, axis, n):
    return [shifted(v, axis, k, n) for v, k in zip(values, SHIFTS[1:], strict=True)]


def gather(value, axis, n):
    mine = [value] + [shifted(value, axis, k, n) for k in GATHER_SHIFTS[1:]]
    return mine + [swap(v) for v in mine]


def on_device(tile_values, tile_rows, tile_cols, tile_count, start_panel):
    tiles = tile_values[0, 0, 0]
    rows = tile_rows[0, 0, 0]
    cols = tile_cols[0, 0, 0]
    count = tile_count[0, 0]
    ids = jnp.stack([lax.axis_index(a) for a in ("layer", "x", "col")]).astype(jnp.int32)
    start = start_panel.reshape(DTILES, TILE, RANK)
    quarter = CTILES // 2 // NCOL

    keep, send, tiles = first_pass(rows, cols, count, ids, tiles, start)
    own, *sends = pair_sum(ids, keep, swap(send), COL, NCOL, quarter, "first_pair")
    by_col, col_numbers = sort_list(rows, cols, count, ids, own, False, "sort_by_col")
    part = four_sum(caller_kernel, col_numbers, own, exchange(sends, "col", NCOL), "first_sum")
    parts = gather(part, "col", NCOL)

    send, panel = send_part(by_col, col_numbers, ids, tiles, parts, False, COL, "back_send")
    got = swap(send)
    [keep] = keep_part(by_col, col_numbers, tiles, panel, False, [], "back_keep")
    own, *sends = pair_sum(ids, keep, got, XPOS, NX, NZ, "back_pair")
    by_row, row_numbers = sort_list(rows, cols, count, ids, own, True, "sort_by_row")
    part = four_sum(row_kernel, row_numbers, own, exchange(sends, "x", NX), "back_sum")
    got = lax.all_to_all(part, "z", split_axis=0, concat_axis=0, tiled=True)
    share, copies = pl.pallas_call(
        share_kernel,
        in_specs=[VMEM],
        out_specs=[VMEM, VMEM],
        out_shape=[jax.ShapeDtypeStruct((TILE, RANK), F32), tiles_of(NZ, BF16)],
        compiler_params=PARAMS,
        name="share_sum",
    )(got)
    part = lax.all_to_all(copies, "z", split_axis=0, concat_axis=0, tiled=True)
    parts = gather(part, "x", NX)

    send, panel = send_part(by_row, row_numbers, ids, tiles, parts, True, XPOS, "last_send")
    got = swap(send)
    keep, squares = keep_part(
        by_row, row_numbers, tiles, panel, True, [jax.ShapeDtypeStruct((TILE // 4, RANK), F32)], "last_keep"
    )
    chunk = jax.ShapeDtypeStruct((quarter * TILE + 16, RANK), BF16)
    own, *sends = pl.pallas_call(
        last_pair_kernel,
        in_specs=[SMEM, VMEM, VMEM, VMEM],
        out_specs=[VMEM] * NCOL,
        out_shape=[tiles_of(quarter, F32)] + [chunk] * (NCOL - 1),
        compiler_params=PARAMS,
        name="last_pair",
    )(ids, keep, got, squares)
    got = exchange(sends, "col", NCOL)
    caller, dest = pl.pallas_call(
        final_kernel,
        in_specs=[VMEM] * 6,
        out_specs=[VMEM, VMEM],
        out_shape=[
            jax.ShapeDtypeStruct((quarter * TILE, RANK), BF16),
            jax.ShapeDtypeStruct((TILE, RANK), BF16),
        ],
        compiler_params=PARAMS,
        name="final",
    )(own, squares, share, *got)
    return caller[None], dest[None]


def solution(mesh):
    fine = Mesh(mesh.devices.reshape(2, NX, NZ, NCOL), ("layer", "x", "z", "col"))
    row = ("x", "z")
    placed = (
        P("layer", row, "col", None, None, None),
        P("layer", row, "col", None),
        P("layer", row, "col", None),
        P("layer", row, "col"),
        P("col", None),
    )
    return jax.shard_map(
        on_device,
        mesh=fine,
        in_specs=placed,
        out_specs=(P(row, ("layer", "col"), None), P("col", ("layer", "x", "z"), None)),
        check_vma=False,
    )
```

```python
import functools

import jax
import jax.numpy as jnp
from jax import lax
from jax.experimental import pallas as pl
from jax.experimental.pallas import tpu as pltpu
from jax.sharding import Mesh
from jax.sharding import PartitionSpec as P

TILE = 128
RANK = 128
CTILES = 32
DTILES = 64
NX = 4
NZ = 8
NCOL = 4
NDST = 32768
N_SLOTS = 256
SLOT_BITS, ROW_BITS, COL_BITS = 8, 5, 6
BLOCK = 32
UNROLL = 32
STEPS = 8
SORT_STEP = 16
SHIFTS = (0, 2, 1, 3)
GATHER_SHIFTS = (0, 1, 3, 2)
EPS = 1e-06

F32 = jnp.float32
BF16 = jnp.bfloat16
CORE, XPOS, COL = 0, 1, 2

SMEM = pl.BlockSpec(memory_space=pltpu.SMEM)
VMEM = pl.BlockSpec(memory_space=pltpu.VMEM)
HBM = pl.BlockSpec(memory_space=pltpu.HBM)
ANY = pl.BlockSpec(memory_space=pl.ANY)
PARAMS = pltpu.CompilerParams(vmem_limit_bytes=40 * 2**20)


def tiles_of(n, dtype):
    return jax.ShapeDtypeStruct((n, TILE, RANK), dtype)


def each(n, body):
    whole = n // STEPS

    def step(i, carry):
        for j in range(STEPS):
            body(i * STEPS + j)
        return carry

    if whole > 1:
        lax.fori_loop(0, whole, step, 0)
    for i in range(whole * STEPS if whole > 1 else 0, n):
        body(i)


def accumulate(lo, hi, live, order, tiles, panel, acc, by_row, keep):
    dump = acc.shape[0] - 1

    def group(g, carry):
        for j in range(UNROLL):
            k = g * UNROLL + j
            code = order[N_SLOTS - 1 - k] if keep else order[k]
            row, col = (code >> SLOT_BITS) & (CTILES - 1), code >> (SLOT_BITS + ROW_BITS)
            dst, src = (row, col) if by_row else (col, row)
            tile, block = tiles[code & (N_SLOTS - 1)], panel[src]
            a, b = (tile, block) if by_row else (block, tile)
            acc[jnp.where(k < live, dst & (dump - 1), dump)] += jnp.dot(a, b, preferred_element_type=F32)
        return carry

    lax.fori_loop(lo, hi, group, 0)


def groups(n):
    return (n + UNROLL - 1) // UNROLL


def zero(acc):
    def one(i):
        acc[i] = jnp.zeros((TILE, RANK), F32)

    each(acc.shape[0], one)


def narrow(acc, out):
    def one(i):
        out[i] = acc[i].astype(BF16)

    each(out.shape[0], one)


def sort_slots(first, size, rows, cols, live, core, order, by_row, counts):
    bits = ROW_BITS if by_row else COL_BITS

    def several(g, carry):
        sends, keeps = carry
        slots = [first + g * SORT_STEP + j for j in range(SORT_STEP)]
        loaded = [(t, rows[t], cols[t]) for t in slots]
        for t, row, col in loaded:
            code = t + (row << SLOT_BITS) + (col << (SLOT_BITS + ROW_BITS))
            dst = row if by_row else col
            own = jnp.where(jnp.logical_and(t < live, dst >> (bits - 1) == core), 1, 0)
            order[jnp.where(own == 1, N_SLOTS - 1 - keeps, sends)] = code
            sends, keeps = sends + 1 - own, keeps + own
        return sends, keeps

    return lax.fori_loop(0, size // SORT_STEP, several, counts)


def sort_kernel(rows, cols, count, ids, after, order, numbers, *, by_row):
    live = count[0]
    counts = sort_slots(0, N_SLOTS, rows, cols, live, ids[CORE], order, by_row, (0, 0))
    numbers[0] = live - counts[1]
    numbers[1] = counts[1]


def sort_list(rows, cols, count, ids, after, by_row, name):
    words = lambda k: jax.ShapeDtypeStruct((k,), jnp.int32)
    return pl.pallas_call(
        functools.partial(sort_kernel, by_row=by_row),
        in_specs=[SMEM] * 4 + [ANY],
        out_specs=[SMEM, SMEM],
        out_shape=[words(N_SLOTS), words(2)],
        cost_estimate=pl.CostEstimate(flops=2 * 10**9, bytes_accessed=4096, transcendentals=0),
        compiler_params=PARAMS,
        name=name,
    )(rows, cols, count, ids, after)


def place(ids, parts, panel, axis, n, per):
    core, me = ids[CORE], ids[axis]
    for side in range(2):
        base = jnp.where(side == 0, core, 1 - core) * (n * per)
        for k in range(n):
            at = base + lax.rem(me + n - GATHER_SHIFTS[k], n) * per
            part = parts[side * n + k]

            def one(i):
                panel[at + i] = part[i]

            each(per, one)


def accumulate_slots(first, size, dst, src, count, tiles, panel, acc):
    live = count[0]
    left = jnp.clip(live - first, 0, size)

    def group(g, carry):
        for j in range(UNROLL):
            t = first + g * UNROLL + j
            d = jnp.where(t < live, dst[t], CTILES)
            acc[d] += jnp.dot(tiles[t], panel[src[t]], preferred_element_type=F32)
        return carry

    lax.fori_loop(0, (left + UNROLL - 1) // UNROLL, group, 0)


def split(ids, acc, keep, send, half):
    core = ids[CORE]

    def one(i):
        keep[i] = acc[core * half + i]
        send[i] = acc[(1 - core) * half + i].astype(BF16)

    each(half, one)


def first_kernel(dst_hbm, src_hbm, count, ids, tiles_hbm, panel_hbm, keep, send, tiles, dst, src, panel, acc, sems):
    n_blocks = tiles.shape[0] // BLOCK
    lists = [
        pltpu.make_async_copy(dst_hbm, dst, sems.at[0]),
        pltpu.make_async_copy(src_hbm, src, sems.at[1]),
        pltpu.make_async_copy(panel_hbm, panel, sems.at[2]),
    ]
    blocks = [
        pltpu.make_async_copy(
            tiles_hbm.at[pl.ds(i * BLOCK, BLOCK)], tiles.at[pl.ds(i * BLOCK, BLOCK)], sems.at[3 + i]
        )
        for i in range(n_blocks)
    ]
    for copy in lists + blocks:
        copy.start()
    zero(acc)
    for copy in lists:
        copy.wait()
    for i in range(n_blocks):
        blocks[i].wait()
        accumulate_slots(i * BLOCK, BLOCK, dst, src, count, tiles, panel, acc)
    split(ids, acc, keep, send, CTILES // 2)


def in_hbm(value):
    return pltpu.with_memory_space_constraint(value, pltpu.HBM)


def first_pass(rows, cols, count, ids, tiles, start):
    return pl.pallas_call(
        first_kernel,
        in_specs=[HBM, HBM, SMEM, SMEM, HBM, HBM],
        out_specs=[VMEM] * 3,
        out_shape=[tiles_of(CTILES // 2, F32), tiles_of(CTILES // 2, BF16), tiles_of(tiles.shape[0], BF16)],
        scratch_shapes=[
            pltpu.SMEM(rows.shape, jnp.int32),
            pltpu.SMEM(cols.shape, jnp.int32),
            pltpu.VMEM(start.shape, BF16),
            pltpu.VMEM((CTILES + 1, TILE, RANK), F32),
            pltpu.SemaphoreType.DMA((3 + tiles.shape[0] // BLOCK,)),
        ],
        compiler_params=pltpu.CompilerParams(vmem_limit_bytes=40 * 2**20),
        name="first_pass",
    )(*(in_hbm(v) for v in (rows, cols)), count, ids, *(in_hbm(v) for v in (tiles, start)))


def send_kernel(order, numbers, ids, tiles, *refs, by_row, axis, n, per):
    parts, (send, panel, acc) = refs[: 2 * n], refs[2 * n :]
    zero(acc)
    place(ids, parts, panel, axis, n, per)
    sends = numbers[0]
    accumulate(0, groups(sends), sends, order, tiles, panel, acc, by_row, False)
    narrow(acc, send)


def send_part(order, numbers, ids, tiles, parts, by_row, axis, name):
    n = len(parts) // 2
    per = parts[0].shape[0]
    half = (CTILES if by_row else DTILES) // 2
    return pl.pallas_call(
        functools.partial(send_kernel, by_row=by_row, axis=axis, n=n, per=per),
        in_specs=[SMEM] * 3 + [VMEM] * (1 + len(parts)),
        out_specs=[VMEM, VMEM],
        out_shape=[tiles_of(half, BF16), tiles_of(2 * n * per, BF16)],
        scratch_shapes=[pltpu.VMEM((half + 1, TILE, RANK), F32)],
        compiler_params=PARAMS,
        name=name,
    )(order, numbers, ids, tiles, *parts)


def keep_kernel(order, numbers, tiles, panel, keep, *squares, by_row):
    zero(keep)
    keeps = numbers[1]
    accumulate(0, groups(keeps), keeps, order, tiles, panel, keep, by_row, True)
    if squares:

        def one(i, total):
            block = panel[i].astype(F32)
            return total + jnp.sum((block * block).reshape(4, TILE // 4, RANK), axis=0)

        squares[0][...] = lax.fori_loop(0, DTILES, one, jnp.zeros((TILE // 4, RANK), F32))


def keep_part(order, numbers, tiles, panel, by_row, extra, name):
    half = (CTILES if by_row else DTILES) // 2
    work = 2 * N_SLOTS * TILE * TILE * RANK
    return pl.pallas_call(
        functools.partial(keep_kernel, by_row=by_row),
        in_specs=[SMEM, SMEM, VMEM, VMEM],
        out_specs=[VMEM] * (1 + len(extra)),
        out_shape=[tiles_of(half + 1, F32)] + extra,
        compiler_params=PARAMS,
        cost_estimate=pl.CostEstimate(flops=work, bytes_accessed=10 * 2**20, transcendentals=0),
        name=name,
    )(order, numbers, tiles, panel)


def pair_kernel(ids, keep, got, own, *sends, axis, n, per):
    me = ids[axis]
    for k in range(n):
        base = lax.rem(me + SHIFTS[k], n) * per

        def one(i):
            total = keep[base + i] + got[base + i].astype(F32)
            if k == 0:
                own[i] = total
            else:
                sends[k - 1][i] = total.astype(BF16)

        each(per, one)


def pair_sum(ids, keep, got, axis, n, per, name):
    return pl.pallas_call(
        functools.partial(pair_kernel, axis=axis, n=n, per=per),
        in_specs=[SMEM, VMEM, VMEM],
        out_specs=[VMEM] * n,
        out_shape=[tiles_of(per, F32)] + [tiles_of(per, BF16)] * (n - 1),
        compiler_params=PARAMS,
        name=name,
    )(ids, keep, got)


def caller_kernel(sorted_first, own, a, b, c, out):
    def one(i):
        total = own[i] + a[i].astype(F32) + b[i].astype(F32) + c[i].astype(F32)
        out[i] = total.astype(BF16).astype(F32).T.astype(BF16)

    each(own.shape[0], one)


def row_kernel(sorted_first, own, a, b, c, out):
    def one(i):
        total = own[i] + a[i].astype(F32) + b[i].astype(F32) + c[i].astype(F32)
        out[i] = total.astype(BF16)

    each(own.shape[0], one)


def four_sum(kernel, sorted_first, own, got, name):
    return pl.pallas_call(
        kernel,
        in_specs=[ANY] + [VMEM] * 4,
        out_specs=VMEM,
        out_shape=tiles_of(own.shape[0], BF16),
        compiler_params=PARAMS,
        name=name,
    )(sorted_first, own, *got)


def share_kernel(got, share, copies):
    total = got[0].astype(F32)
    for k in range(1, NZ):
        total += got[k].astype(F32)
    total = total.T
    share[...] = total
    for k in range(NZ):
        copies[k] = total.astype(BF16)


def last_pair_kernel(ids, keep, got, squares, own, *sends):
    me = ids[COL]
    per = CTILES // 2 // NCOL
    total = jnp.sum(squares[...], axis=0, keepdims=True)
    high = total.astype(BF16).astype(F32)
    middle = (total - high).astype(BF16).astype(F32)
    low = total - high - middle
    row = lax.broadcasted_iota(jnp.int32, (16, RANK), 0)
    coded = jnp.where(row == 0, high, jnp.where(row == 1, middle, jnp.where(row == 2, low, 0.0)))
    for k in range(NCOL):
        base = lax.rem(me + SHIFTS[k], NCOL) * per
        if k:
            sends[k - 1][pl.ds(per * TILE, 16), :] = coded.astype(BF16)
        for i in range(per):
            part = keep[base + i] + got[base + i].astype(F32)
            if k == 0:
                own[i] = part
            else:
                sends[k - 1][pl.ds(i * TILE, TILE), :] = part.astype(BF16)


def final_kernel(own, squares, share, a, b, c, caller, dest):
    per = CTILES // 2 // NCOL
    total = jnp.sum(squares[...], axis=0, keepdims=True)
    for got in (a, b, c):
        total += jnp.sum(got[pl.ds(per * TILE, 16), :].astype(F32), axis=0, keepdims=True)
    scale = lax.rsqrt(total / NDST + EPS)
    dest[...] = (share[...] * scale).astype(BF16)
    for i in range(per):
        at = pl.ds(i * TILE, TILE)
        part = own[i] + a[at, :].astype(F32) + b[at, :].astype(F32) + c[at, :].astype(F32)
        caller[at, :] = (part * scale).astype(BF16)


def shifted(value, axis, k, n):
    return lax.ppermute(value, axis, [(i, (i + k) % n) for i in range(n)])


def swap(value):
    return lax.ppermute(value, "layer", [(0, 1), (1, 0)])


def exchange(values, axis, n):
    return [shifted(v, axis, k, n) for v, k in zip(values, SHIFTS[1:], strict=True)]


def gather(value, axis, n):
    mine = [value] + [shifted(value, axis, k, n) for k in GATHER_SHIFTS[1:]]
    return mine + [swap(v) for v in mine]


def on_device(tile_values, tile_rows, tile_cols, tile_count, start_panel):
    tiles = tile_values[0, 0, 0]
    rows = tile_rows[0, 0, 0]
    cols = tile_cols[0, 0, 0]
    count = tile_count[0, 0]
    ids = jnp.stack([lax.axis_index(a) for a in ("layer", "x", "col")]).astype(jnp.int32)
    start = start_panel.reshape(DTILES, TILE, RANK)
    quarter = CTILES // 2 // NCOL

    keep, send, tiles = first_pass(rows, cols, count, ids, tiles, start)
    own, *sends = pair_sum(ids, keep, swap(send), COL, NCOL, quarter, "first_pair")
    by_col, col_numbers = sort_list(rows, cols, count, ids, own, False, "sort_by_col")
    part = four_sum(caller_kernel, col_numbers, own, exchange(sends, "col", NCOL), "first_sum")
    parts = gather(part, "col", NCOL)

    send, panel = send_part(by_col, col_numbers, ids, tiles, parts, False, COL, "back_send")
    got = swap(send)
    [keep] = keep_part(by_col, col_numbers, tiles, panel, False, [], "back_keep")
    own, *sends = pair_sum(ids, keep, got, XPOS, NX, NZ, "back_pair")
    by_row, row_numbers = sort_list(rows, cols, count, ids, own, True, "sort_by_row")
    part = four_sum(row_kernel, row_numbers, own, exchange(sends, "x", NX), "back_sum")
    got = lax.all_to_all(part, "z", split_axis=0, concat_axis=0, tiled=True)
    share, copies = pl.pallas_call(
        share_kernel,
        in_specs=[VMEM],
        out_specs=[VMEM, VMEM],
        out_shape=[jax.ShapeDtypeStruct((TILE, RANK), F32), tiles_of(NZ, BF16)],
        compiler_params=PARAMS,
        name="share_sum",
    )(got)
    part = lax.all_to_all(copies, "z", split_axis=0, concat_axis=0, tiled=True)
    parts = gather(part, "x", NX)

    send, panel = send_part(by_row, row_numbers, ids, tiles, parts, True, XPOS, "last_send")
    got = swap(send)
    keep, squares = keep_part(
        by_row, row_numbers, tiles, panel, True, [jax.ShapeDtypeStruct((TILE // 4, RANK), F32)], "last_keep"
    )
    chunk = jax.ShapeDtypeStruct((quarter * TILE + 16, RANK), BF16)
    own, *sends = pl.pallas_call(
        last_pair_kernel,
        in_specs=[SMEM, VMEM, VMEM, VMEM],
        out_specs=[VMEM] * NCOL,
        out_shape=[tiles_of(quarter, F32)] + [chunk] * (NCOL - 1),
        compiler_params=PARAMS,
        name="last_pair",
    )(ids, keep, got, squares)
    got = exchange(sends, "col", NCOL)
    caller, dest = pl.pallas_call(
        final_kernel,
        in_specs=[VMEM] * 6,
        out_specs=[VMEM, VMEM],
        out_shape=[
            jax.ShapeDtypeStruct((quarter * TILE, RANK), BF16),
            jax.ShapeDtypeStruct((TILE, RANK), BF16),
        ],
        compiler_params=PARAMS,
        name="final",
    )(own, squares, share, *got)
    return caller[None], dest[None]


def solution(mesh):
    fine = Mesh(mesh.devices.reshape(2, NX, NZ, NCOL), ("layer", "x", "z", "col"))
    row = ("x", "z")
    placed = (
        P("layer", row, "col", None, None, None),
        P("layer", row, "col", None),
        P("layer", row, "col", None),
        P("layer", row, "col"),
        P("col", None),
    )
    return jax.shard_map(
        on_device,
        mesh=fine,
        in_specs=placed,
        out_specs=(P(row, ("layer", "col"), None), P("col", ("layer", "x", "z"), None)),
        check_vma=False,
    )
```
